32 devices in a mesh: groups: 2 (over x), tok: 16 (over z, y, core).
Axes of the slice: x: 2, y: 2, z: 4, core: 2. Of those that a mesh axis runs over, the one named last changes fastest.
Arguments:
- tokens: bfloat16 [4096, 3072], P(('groups', 'tok')), parts along dimension 0, may hold values from -6 to 6
- routes: int32 [4096, 2], P(('groups', 'tok')), parts along dimension 0, may hold values from 0 to 7, all different within a row; in each aligned block of 128 rows (0 to 127, 128 to 255, ...) at most 40 rows name the same one
- weights: bfloat16 [32768, 3072], P(('groups', 'tok')), parts along dimension 0, may hold values from -0.109375 to 0.109375
Outputs:
- whitened: bfloat16 [32768, 3072], P(('groups', 'tok')), parts along dimension 0
The draws below stay inside these ranges and needn't reach their ends.
There are 2 independent parts, one for each index of `groups`. The reference program is written for one: setup_inputs(seed, part) draws one part's arguments, and reference() takes and returns one part's arrays. A program takes and returns all parts, laid end to end along the dimension named above; each array names one. Nothing has to cross between parts.
Inputs may be any that keep to these rules, and one draw needn't show every extreme that they name: `routes`: each token names 2 different experts. Within the tokens of one device no expert is named more than 40 times, and in every draw some expert is named exactly 40 times by the tokens of some device.
All inputs are finite; a program needn't handle non-finite values.
Results may differ from the reference program's by a relative error of at most 0.0064.
The reference program's roundings to bfloat16 on the way (of `expert_rows` and `lower`) count: a program that leaves them out, or rounds other values in their place, can miss the bound.
Values may be sent and summed in bfloat16 or wider, within the bound.
No kernel may reach another device: no remote copies, remote signals or barrier semaphores. Data moves between devices by JAX's collectives and lax.ppermute only.
A program may use at most 256 MiB of HBM per device.

```python
import math
import jax
import jax.numpy as jnp
import numpy as np
from jax import lax

D = 3072
E = 8
TOP = 2
FF_DEV = 1024
NB = 4
TOK_DEV = 128
MOST = 40
FF = 2048
TOKENS = 2048
N_TOK = 16


def level_of(key, shape, shards, smallest, largest):
    loudness, own = 1.0, jax.random.fold_in(key, 6)
    for axis_at, parts in shards:
        draws = jnp.exp(jax.random.uniform(jax.random.fold_in(own, axis_at), (parts,), jnp.float32, smallest / len(shards), largest / len(shards)))
        loudness = loudness * jnp.repeat(draws, shape[axis_at] // parts).reshape([-1 if axis == axis_at else 1 for axis in range(len(shape))])
    return loudness


def assign_block(own_key, own, number, rows, count, top, reach, skew):
    ranking = jax.random.permutation(own_key, count)
    packed, common = shares(count, rows * top, reach, skew, True), shares(count, rows * top, reach, skew, False)
    places = jnp.arange(count)

    def named(sizes, offset_by):
        used = int((sizes > 0).sum())
        fixed = max(1, used // 4)
        shifted = fixed + (places - fixed + offset_by * (used - fixed)) % max(1, count - fixed)
        return jnp.zeros((count,), jnp.int32).at[ranking[jnp.where(places < fixed, places, shifted)]].set(jnp.asarray(sizes, jnp.int32))

    sizes = jnp.where(number % 4 == 0, named(packed, number // 4), named(common, number - number // 4 - 1))
    mixed = jax.random.permutation(jax.random.fold_in(own, 3), count)
    donor, taker = mixed[0:count // 2 * 2:2], mixed[1:count // 2 * 2:2]
    margin = jnp.minimum(sizes[donor] - 1, reach - sizes[taker]) // 2
    margin = jnp.where((donor == ranking[0]) | (taker == ranking[0]) | (sizes[taker] == 0), 0, jnp.maximum(margin, 0))
    shifted = jax.random.randint(jax.random.fold_in(own, 4), (count // 2,), 0, 1 << 20) % (margin + 1)
    sizes = sizes.at[donor].add(-shifted).at[taker].add(shifted)
    members = jnp.searchsorted(jnp.cumsum(sizes), jnp.arange(rows * top), side="right").astype(jnp.int32)
    grid = members.reshape(top, rows).T
    grid = grid[jax.random.permutation(jax.random.fold_in(own, 1), rows)]
    offset_by = jax.random.randint(jax.random.fold_in(own, 2), (rows, 1), 0, top)
    return jnp.take_along_axis(grid, (jnp.arange(top)[None, :] + offset_by) % top, axis=1)


def shares(number_of, total, most, lean, full):
    portions = [(1 << 20) // math.isqrt(standing ** lean) + 1 for standing in range(1, number_of + 1)]
    largest = most if full else min(most, max(-(-total // number_of), total * portions[0] // sum(portions)))
    least = 1 if total - largest >= number_of - 1 else 0
    given, spare = [largest] + [least] * (number_of - 1), total - largest - least * (number_of - 1)
    while spare > 0:
        free = [i for i in range(1, number_of) if given[i] < largest] or [i for i in range(1, number_of) if given[i] < most]
        mass, remaining = sum([portions[i] for i in free]), spare
        for i in free:
            addition = min(most - given[i], max(1, remaining * portions[i] // mass), spare)
            given[i] = given[i] + addition
            spare = spare - addition
    return np.array(given)


def scatter_about(rng, shape, deviation, bound, shards=(), kind=jnp.bfloat16):
    level = level_of(rng, shape, shards, -0.22, 0.18) if shards else 1.0
    entries = jax.random.normal(rng, shape, jnp.float32) * deviation * level
    return jnp.minimum(jnp.maximum(entries, -bound), bound).astype(kind)


def setup_inputs(seed: int = 0, part: int = 0) -> dict:
    key_list = jax.random.split(jax.random.key(seed), 4)
    part_splits = jax.random.split(jax.random.fold_in(key_list[3], part), 4)
    tokens = scatter_about(part_splits[0], (TOKENS, D), 1.0, 6.0, ((0, 16),))
    routes_keys = jax.random.split(jax.random.fold_in(part_splits[1], 1), TOKENS // TOK_DEV)
    routes_turns = jax.random.permutation(jax.random.fold_in(part_splits[1], 3), TOKENS // TOK_DEV)
    routes = jax.vmap(lambda own, number: assign_block(jax.random.fold_in(part_splits[1], 2), own, number, TOK_DEV, E, TOP, MOST, 2))(routes_keys, routes_turns).reshape((TOKENS, TOP))
    weights = scatter_about(part_splits[2], (E * FF, D), D ** -0.5, 0.109375, ((0, 16),))
    return {"tokens": tokens, "routes": routes, "weights": weights}


damping = 256.0

def reference(tokens, routes, weights):
    slices = N_TOK // E
    hidden = FF_DEV * slices
    cap_rows = N_TOK * MOST
    band_width = D // NB
    results = []
    for expert in range(E):
        hit_count = jnp.sum((routes == expert).astype(jnp.int32), axis=1)
        row_index = jnp.nonzero(hit_count > 0, size=cap_rows, fill_value=0)[0].astype(jnp.int32)
        valid_rows = jnp.arange(cap_rows, dtype=jnp.int32) < jnp.sum(hit_count)
        expert_rows = jnp.where(valid_rows[:, None], tokens[row_index], jnp.zeros((), tokens.dtype))
        gram_matrix = lax.dot_general(expert_rows.astype(jnp.float32), expert_rows.astype(jnp.float32), (((0,), (0,)), ((), ())), preferred_element_type=jnp.float32)
        lower_bf = jnp.zeros((D, D), jnp.bfloat16)
        for section in range(NB):
            lo_col = section * band_width
            hi_col = lo_col + band_width
            column_block = gram_matrix[lo_col:, lo_col:hi_col]
            if section > 0:
                column_block = column_block - lax.dot_general(lower_bf[lo_col:, :lo_col].astype(jnp.float32), lower_bf[lo_col:hi_col, :lo_col].astype(jnp.float32), (((1,), (1,)), ((), ())), preferred_element_type=jnp.float32)
            diag_block = column_block[:band_width] + damping * jnp.eye(band_width, dtype=jnp.float32)
            diag_factor = jnp.linalg.cholesky(diag_block)
            stacked = diag_factor
            if section + 1 < NB:
                below_rows = lax.linalg.triangular_solve(diag_factor, column_block[band_width:], left_side=False, lower=True, transpose_a=True)
                stacked = jnp.concatenate([diag_factor, below_rows], 0)
            lower_bf = lower_bf.at[lo_col:, lo_col:hi_col].set(stacked.astype(jnp.bfloat16))
        expert_weight = weights[expert * hidden:(expert + 1) * hidden]
        results.append(jnp.dot(expert_weight.astype(jnp.float32), lower_bf.astype(jnp.float32), preferred_element_type=jnp.float32).astype(jnp.bfloat16))
    return jnp.concatenate(results, 0)
```

```python
import functools

import jax
import jax.numpy as jnp
from jax import lax
from jax.experimental import pallas as pl
from jax.experimental.pallas import tpu as pltpu
from jax.sharding import PartitionSpec as P

E = 8
NB = 4
BLK = 128
ROWS = 8
VMEM = 56 * 1024 * 1024

damping = 256.0

f32 = jnp.float32
bf16 = jnp.bfloat16


def dot(a, b):
    return jnp.dot(a, b, preferred_element_type=f32)


def dot_t(a, b):
    return lax.dot_general(a, b, (((0,), (0,)), ((), ())), preferred_element_type=f32)


def split(a):
    high = a.astype(bf16)
    return high, (a - high.astype(f32)).astype(bf16)


def dot3(a, b):
    (ah, al), (bh, bl) = a, b
    return dot(ah, bh) + (dot(ah, bl) + dot(al, bh))


def factor_block(load, store_u, store_v):
    groups = BLK // ROWS
    sub = lax.broadcasted_iota(jnp.int32, (ROWS, BLK), 0)
    lane = lax.broadcasted_iota(jnp.int32, (ROWS, BLK), 1)

    def row(x, k):
        return jnp.broadcast_to(x[k : k + 1, :], (ROWS, BLK))

    def col(x, j):
        return jnp.broadcast_to(x[:, j : j + 1], (ROWS, BLK))

    a_rows = [load(g) for g in range(groups)]
    i_rows = [(lane == sub + ROWS * g).astype(f32) for g in range(groups)]
    for p in range(groups):
        base = ROWS * p
        cols = [col(a_rows[p], base + c) for c in range(ROWS)]
        later = {g: [col(a_rows[g], base + c) for c in range(ROWS)] for g in range(p + 1, groups)}
        a, i = a_rows[p], i_rows[p]
        u = jnp.zeros((ROWS, BLK), f32)
        v = jnp.zeros((ROWS, BLK), f32)
        for k in range(0, ROWS, 2):
            here, next_ = sub == k, sub == k + 1
            pair = here | next_
            p00, p01, p11 = row(cols[k], k), row(cols[k], k + 1), row(cols[k + 1], k + 1)
            det = p00 * p11 - p01 * p01
            r = pltpu.reciprocal(det, approx=True)
            f0 = jnp.where(here, -1.0, jnp.where(next_, 0.0, cols[k]))
            f1 = jnp.where(next_, -1.0, jnp.where(here, 0.0, cols[k + 1]))

            def eliminate(t):
                t0, t1 = row(t, k), row(t, k + 1)
                m0, m1 = p11 * t0 - p01 * t1, p00 * t1 - p01 * t0
                return jnp.where(pair, 0.0, t) - (f0 * m0 + f1 * m1) * r, t0, m1

            s0, s1 = lax.rsqrt(p00), lax.rsqrt(p00 * det)
            a, t0, m1 = eliminate(a)
            u = jnp.where(here, t0 * s0, jnp.where(next_, m1 * s1, u))
            i, t0, m1 = eliminate(i)
            v = jnp.where(here, t0 * s0, jnp.where(next_, m1 * s1, v))
            for c in range(k + 2, ROWS):
                cols[c] = eliminate(cols[c])[0]
        store_u(p, jnp.where(lane >= sub + base, u, 0.0))
        store_v(p, v)
        a_k = [row(a, k) for k in range(ROWS)]
        i_k = [row(i, k) for k in range(ROWS)]
        for g in range(p + 1, groups):
            w = later[g]

            def total(rows):
                t = [w[k] * rows[k] for k in range(ROWS)]
                while len(t) > 1:
                    t = [x + y for x, y in zip(t[::2], t[1::2])]
                return t[0]

            a_rows[g] = a_rows[g] - total(a_k)
            i_rows[g] = i_rows[g] - total(i_k)


def diag_kernel(blocks, has_prev, *refs):
    if has_prev:
        x_ref, prev_ref, u_ref, uh_ref, ul_ref, vh_ref, vl_ref, s_ref, f_ref, v_ref = refs
    else:
        x_ref, u_ref, uh_ref, ul_ref, vh_ref, vl_ref, s_ref, f_ref, v_ref = refs
    width = blocks * BLK
    row_at = lax.broadcasted_iota(jnp.int32, (BLK, width), 0)
    col_at = lax.broadcasted_iota(jnp.int32, (BLK, width), 1)
    for b in range(blocks):
        mine = slice(b * BLK, (b + 1) * BLK)
        s = dot_t(x_ref[:, mine], x_ref[...])
        if has_prev:
            s = s - dot_t(prev_ref[:, mine], prev_ref[...])
        s_ref[b] = s + jnp.where(col_at == row_at + b * BLK, damping, 0.0)

    def step(b, _):
        mine = pl.ds(pl.multiple_of(b * BLK, BLK), BLK)

        def load(g):
            return s_ref[b, ROWS * g : ROWS * (g + 1), mine]

        def store_u(g, u):
            f_ref[ROWS * g : ROWS * (g + 1), :] = u

        def store_v(g, v):
            v_ref[ROWS * g : ROWS * (g + 1), :] = v

        factor_block(load, store_u, store_v)
        vh, vl = split(v_ref[...])
        vh_ref[b] = vh
        vl_ref[b] = vl
        u = dot3((vh, vl), split(s_ref[b]))
        s_ref[b] = jnp.where(col_at >= (b + 1) * BLK, u, 0.0)
        s_ref[b, :, mine] = f_ref[...]
        uh, ul = split(s_ref[b])

        def update(later, _):
            at = pl.ds(pl.multiple_of(later * BLK, BLK), BLK)
            left = split(s_ref[b, :, at].T)
            s_ref[later] = s_ref[later] - dot3(left, (uh, ul))
            return 0

        lax.fori_loop(b + 1, blocks, update, 0)
        return 0

    lax.fori_loop(0, blocks, step, 0)
    for b in range(blocks):
        uh, ul = split(s_ref[b])
        u_ref[b * BLK : (b + 1) * BLK, :] = uh
        uh_ref[:, b * BLK : (b + 1) * BLK] = uh.T
        ul_ref[:, b * BLK : (b + 1) * BLK] = ul.T


def diag(x, prev):
    width = x.shape[1]
    blocks = width // BLK
    square = jax.ShapeDtypeStruct((width, width), bf16)
    small = jax.ShapeDtypeStruct((blocks, BLK, BLK), bf16)
    operands = [x] if prev is None else [x, prev]
    return pl.pallas_call(
        functools.partial(diag_kernel, blocks, prev is not None),
        out_shape=[square, square, square, small, small],
        in_specs=[pl.BlockSpec(memory_space=pltpu.VMEM)] * len(operands),
        out_specs=[pl.BlockSpec(memory_space=pltpu.VMEM)] * 5,
        scratch_shapes=[
            pltpu.VMEM((blocks, BLK, width), f32),
            pltpu.VMEM((BLK, BLK), f32),
            pltpu.VMEM((BLK, BLK), f32),
        ],
        compiler_params=pltpu.CompilerParams(vmem_limit_bytes=VMEM),
        cost_estimate=pl.CostEstimate(
            flops=20_000_000_000, bytes_accessed=4 * width * width, transcendentals=0
        ),
        name="diag_factor",
    )(*operands)


def rows_kernel(blocks, has_prev, *refs):
    if has_prev:
        x_ref, xt_ref, p_ref, pt_ref, lh_ref, ll_ref, vh_ref, vl_ref, out_ref, s_ref, h_ref, l_ref = refs
    else:
        x_ref, xt_ref, lh_ref, ll_ref, vh_ref, vl_ref, out_ref, s_ref, h_ref, l_ref = refs
    s_ref[...] = dot_t(x_ref[...], xt_ref[...])
    if has_prev:
        s_ref[...] = s_ref[...] - dot_t(p_ref[...], pt_ref[...])
    for b in range(blocks):
        mine = slice(b * BLK, (b + 1) * BLK)
        s = s_ref[mine, :]
        if b:
            done = slice(0, b * BLK)
            s = s - dot3(
                (lh_ref[mine, done], ll_ref[mine, done]), (h_ref[done, :], l_ref[done, :])
            )
        u = dot3((vh_ref[b], vl_ref[b]), split(s))
        h, l = split(u)
        h_ref[mine, :] = h
        l_ref[mine, :] = l
        out_ref[mine, :] = h


def rows(x, x_later, prev, prev_later, factors):
    width, columns = x.shape[1], x_later.shape[1]
    blocks, tile = width // BLK, width // 2

    def whole(a):
        return pl.BlockSpec(a.shape, lambda i, n=a.ndim: (0,) * n)

    def tiled(a):
        return pl.BlockSpec((a.shape[0], tile), lambda i: (0, i))

    operands, specs = [x, x_later], [whole(x), tiled(x_later)]
    if prev is not None:
        operands += [prev, prev_later]
        specs += [whole(prev), tiled(prev_later)]
    operands += factors
    specs += [whole(a) for a in factors]
    return pl.pallas_call(
        functools.partial(rows_kernel, blocks, prev is not None),
        out_shape=jax.ShapeDtypeStruct((width, columns), bf16),
        grid=(columns // tile,),
        in_specs=specs,
        out_specs=pl.BlockSpec((width, tile), lambda i: (0, i)),
        scratch_shapes=[
            pltpu.VMEM((width, tile), f32),
            pltpu.VMEM((width, tile), bf16),
            pltpu.VMEM((width, tile), bf16),
        ],
        compiler_params=pltpu.CompilerParams(vmem_limit_bytes=VMEM),
        cost_estimate=pl.CostEstimate(
            flops=8 * width * width * columns, bytes_accessed=6 * width * columns, transcendentals=0
        ),
        name="right_rows",
    )(*operands)


def local(tokens, routes, weights):
    devices = lax.axis_size("tok")
    me = lax.axis_index("tok")
    slices = devices // E
    tok_rows, features = tokens.shape
    most_rows = tok_rows * 5 // 16
    slot_cap = most_rows // slices
    width = features // NB

    picked = routes.reshape(-1)
    onehot = (picked[:, None] == jnp.arange(E, dtype=jnp.int32)[None, :]).astype(jnp.int32)
    before = jnp.cumsum(onehot, axis=0) - onehot
    ranked = jnp.sum(before * onehot, axis=1)
    device = picked * slices + ranked % slices
    place = ranked // slices
    slots = devices * slot_cap

    def pack(target, values):
        table = (target[None, :] == jnp.arange(slots, dtype=jnp.int32)[:, None]).astype(f32)
        table = jnp.sum(table.reshape(slots, tok_rows, 2), axis=2).astype(bf16)
        return dot(table, values).astype(bf16)

    def collect(piece):
        for bit in range(slices.bit_length() - 1):
            route = [(d, d ^ 1 << bit) for d in range(devices)]
            piece = jnp.concatenate([piece, lax.ppermute(piece, "tok", route)], 0)
        return piece

    first = pack(device * slot_cap + place, tokens[:, :width])
    rest = pack((device ^ me) * slot_cap + place, tokens[:, width:])
    first = lax.all_to_all(first, "tok", split_axis=0, concat_axis=0, tiled=True)
    slot = jnp.arange(slots, dtype=jnp.int32)
    source = (slot // slot_cap ^ me) * slot_cap + slot % slot_cap
    first = dot((source[:, None] == slot[None, :]).astype(bf16), first).astype(bf16)
    first, rest = lax.optimization_barrier((first, rest))
    pieces = [rest[:slot_cap]]
    for flip in range(1, devices):
        route = [(d, d ^ flip) for d in range(devices)]
        pieces.append(lax.ppermute(rest[flip * slot_cap : (flip + 1) * slot_cap], "tok", route))
    x = [collect(first)]
    factors = diag(x[0], None)
    rest = collect(jnp.concatenate(pieces, 0))

    upper = [[factors[0]]]
    upper[0].append(rows(x[0], rest, None, None, factors[1:]))
    for band in range(1, NB):
        at = (band - 1) * width
        x_band = rest[:, at : at + width]
        above = [upper[b][1][:, (band - 1 - b) * width : (band - b) * width] for b in range(band)]
        prev = jnp.concatenate(above, 0)
        factors = diag(x_band, prev)
        upper.append([factors[0]])
        if band + 1 < NB:
            later = [upper[b][1][:, (band - b) * width :] for b in range(band)]
            upper[band].append(
                rows(x_band, rest[:, at + width :], prev, jnp.concatenate(later, 0), factors[1:])
            )

    outputs = []
    for band in range(NB):
        total = lax.dot_general(
            weights[:, band * width : (band + 1) * width],
            upper[band][0],
            (((1,), (1,)), ((), ())),
            preferred_element_type=f32,
        )
        if band + 1 < NB:
            total = total + lax.dot_general(
                weights[:, (band + 1) * width :],
                upper[band][1],
                (((1,), (1,)), ((), ())),
                preferred_element_type=f32,
            )
        outputs.append(total.astype(bf16))
    return jnp.concatenate(outputs, 1)


def solution(mesh):
    spec = P(("groups", "tok"), None)
    return jax.shard_map(
        local, mesh=mesh, in_specs=(spec, spec, spec), out_specs=spec, check_vma=False
    )
```

```python
import functools

import jax
import jax.numpy as jnp
from jax import lax
from jax.experimental import pallas as pl
from jax.experimental.pallas import tpu as pltpu
from jax.sharding import PartitionSpec as P

E = 8
NB = 4
BLK = 128
ROWS = 8
VMEM = 56 * 1024 * 1024

damping = 256.0

f32 = jnp.float32
bf16 = jnp.bfloat16


def dot(a, b):
    return jnp.dot(a, b, preferred_element_type=f32)


def dot_t(a, b):
    return lax.dot_general(a, b, (((0,), (0,)), ((), ())), preferred_element_type=f32)


def split(a):
    high = a.astype(bf16)
    return high, (a - high.astype(f32)).astype(bf16)


def dot3(a, b):
    (ah, al), (bh, bl) = a, b
    return dot(ah, bh) + (dot(ah, bl) + dot(al, bh))


def factor_block(load, store_u, store_v):
    groups = BLK // ROWS
    sub = lax.broadcasted_iota(jnp.int32, (ROWS, BLK), 0)
    lane = lax.broadcasted_iota(jnp.int32, (ROWS, BLK), 1)

    def row(x, k):
        return jnp.broadcast_to(x[k : k + 1, :], (ROWS, BLK))

    def col(x, j):
        return jnp.broadcast_to(x[:, j : j + 1], (ROWS, BLK))

    a_rows = [load(g) for g in range(groups)]
    for p in range(groups):
        base = ROWS * p
        panel = (lane >= base) & (lane < base + ROWS)
        cols = [col(a_rows[p], base + c) for c in range(ROWS)]
        s = a_rows[p]
        a = jnp.where(panel, (lane == sub + base).astype(f32), s)
        u = jnp.zeros((ROWS, BLK), f32)
        v = jnp.zeros((ROWS, BLK), f32)
        for k in range(0, ROWS, 2):
            here, next_ = sub == k, sub == k + 1
            pair = here | next_
            p00, p01, p11 = row(cols[k], k), row(cols[k], k + 1), row(cols[k + 1], k + 1)
            det = p00 * p11 - p01 * p01
            r = pltpu.reciprocal(det, approx=True)
            f0 = jnp.where(here, -1.0, jnp.where(next_, 0.0, cols[k]))
            f1 = jnp.where(next_, -1.0, jnp.where(here, 0.0, cols[k + 1]))

            def eliminate(t):
                t0, t1 = row(t, k), row(t, k + 1)
                m0, m1 = p11 * t0 - p01 * t1, p00 * t1 - p01 * t0
                return jnp.where(pair, 0.0, t) - (f0 * m0 + f1 * m1) * r, t0, m1

            s0, s1 = lax.rsqrt(p00), lax.rsqrt(p00 * det)
            for c in range(k + 2, ROWS):
                cols[c] = eliminate(cols[c])[0]
            a, t0, m1 = eliminate(a)
            v = jnp.where(here, t0 * s0, jnp.where(next_, m1 * s1, v))
            s, t0, m1 = eliminate(s)
            u = jnp.where(here, t0 * s0, jnp.where(next_, m1 * s1, u))
        store_u(p, jnp.where(lane >= sub + base, u, 0.0))
        store_v(p, jnp.where(lane < base + ROWS, v, 0.0))
        a_k = [row(a, k) for k in range(ROWS)]
        for g in range(p + 1, groups):
            t = [col(a_rows[g], base + k) * a_k[k] for k in range(ROWS)]
            while len(t) > 1:
                t = [x + y for x, y in zip(t[::2], t[1::2])]
            a_rows[g] = jnp.where(panel, 0.0, a_rows[g]) - t[0]


def stack(refs, out_ref):
    at = 0
    for ref in refs:
        out_ref[at : at + ref.shape[0], :] = ref[...]
        at += ref.shape[0]


def diag_kernel(pieces, band, blocks, *refs):
    x_refs, prev_refs, refs = refs[:pieces], refs[pieces : pieces + band], refs[pieces + band :]
    out_ref, lh_ref, ll_ref, vh_ref, vl_ref = refs[:5]
    x_ref, s_ref, d_ref, f_ref, v_ref, uh_ref, ul_ref, both_ref, twice_ref = refs[5:]
    width = blocks * BLK
    row_at = lax.broadcasted_iota(jnp.int32, (BLK, width), 0)
    col_at = lax.broadcasted_iota(jnp.int32, (BLK, width), 1)
    stack(x_refs, x_ref)
    for b in range(blocks):
        mine, on = slice(b * BLK, (b + 1) * BLK), slice(b * BLK, width)
        s = dot_t(x_ref[:, mine], x_ref[:, on])
        for prev_ref in prev_refs:
            s = s - dot_t(prev_ref[:, mine], prev_ref[:, on])
        s_ref[mine, on] = s + jnp.where(col_at[:, on] == row_at[:, on] + b * BLK, damping, 0.0)
    d_ref[...] = s_ref[:BLK, :BLK]

    def block(b):
        return pl.ds(pl.multiple_of(b * BLK, BLK), BLK)

    def step(b, _):
        def load(g):
            return d_ref[ROWS * g : ROWS * (g + 1), :]

        def store_u(g, u):
            f_ref[b, ROWS * g : ROWS * (g + 1), :] = u

        def store_v(g, v):
            v_ref[ROWS * g : ROWS * (g + 1), :] = v

        factor_block(load, store_u, store_v)

        before = jnp.maximum(b - 1, 0)
        u = dot3((vh_ref[before], vl_ref[before]), split(s_ref[block(before), :]))
        uh, ul = split(jnp.where((col_at >= (before + 1) * BLK) & (b > 0), u, 0.0))
        uh_ref[block(before), :] = uh
        ul_ref[block(before), :] = ul
        both_ref[:BLK, :] = uh
        both_ref[BLK:, :] = ul
        twice_ref[:BLK, :] = uh
        twice_ref[BLK:, :] = uh
        for later in range(1, blocks):
            mine, on = slice(later * BLK, (later + 1) * BLK), slice(later * BLK, width)
            s_ref[mine, on] = s_ref[mine, on] - (
                dot_t(both_ref[:, mine], twice_ref[:, on]) + dot_t(both_ref[:BLK, mine], both_ref[BLK:, on])
            )

        v = split(v_ref[...])
        vh_ref[b], vl_ref[b] = v
        after = jnp.minimum(b + 1, blocks - 1)
        u = dot3(v, split(s_ref[block(b), block(after)]))
        d_ref[...] = s_ref[block(after), block(after)] - dot3(split(u.T), split(u))
        return 0

    lax.fori_loop(0, blocks, step, 0)
    uh_ref[width - BLK :, :] = jnp.zeros((BLK, width), bf16)
    ul_ref[width - BLK :, :] = jnp.zeros((BLK, width), bf16)
    for b in range(blocks):
        mine = slice(b * BLK, (b + 1) * BLK)
        uh_ref[mine, mine], ul_ref[mine, mine] = split(f_ref[b])
    out_ref[...] = uh_ref[...]
    for b in range(blocks):
        mine = slice(b * BLK, (b + 1) * BLK)
        lh_ref[:, mine] = uh_ref[mine, :].T
        ll_ref[:, mine] = ul_ref[mine, :].T


def at_block(shape, r, c):
    return pl.BlockSpec(shape, lambda i: (r, c))


def diag(x, above):
    width = x[0][2]
    blocks = width // BLK
    square = jax.ShapeDtypeStruct((width, width), bf16)
    small = jax.ShapeDtypeStruct((blocks, BLK, BLK), bf16)
    count = sum(a.shape[0] for a, _, _ in x)
    operands = [a for a, _, _ in x] + [a for a, _ in above]
    specs = [at_block((a.shape[0], width), 0, c) for a, c, _ in x]
    specs += [at_block((width, width), 0, c) for _, c in above]
    return pl.pallas_call(
        functools.partial(diag_kernel, len(x), len(above), blocks),
        out_shape=[square, square, square, small, small],
        grid=(1,),
        in_specs=specs,
        out_specs=[at_block((width, width), 0, 0)] * 3
        + [pl.BlockSpec(small.shape, lambda i: (0, 0, 0))] * 2,
        scratch_shapes=[
            pltpu.VMEM((count, width), bf16),
            pltpu.VMEM((width, width), f32),
            pltpu.VMEM((BLK, BLK), f32),
            pltpu.VMEM((blocks, BLK, BLK), f32),
            pltpu.VMEM((BLK, BLK), f32),
            pltpu.VMEM((width, width), bf16),
            pltpu.VMEM((width, width), bf16),
            pltpu.VMEM((2 * BLK, width), bf16),
            pltpu.VMEM((2 * BLK, width), bf16),
        ],
        compiler_params=pltpu.CompilerParams(vmem_limit_bytes=VMEM),
        cost_estimate=pl.CostEstimate(
            flops=30_000_000_000, bytes_accessed=8 * width * width, transcendentals=0
        ),
        name="diag_factor",
    )(*operands)


def rows_kernel(pieces, band, blocks, *refs):
    x_refs, later_refs, refs = refs[:pieces], refs[pieces : 2 * pieces], refs[2 * pieces :]
    p_refs, above_refs, refs = refs[:band], refs[band : 2 * band], refs[2 * band :]
    lh_ref, ll_ref, vh_ref, vl_ref, out_ref = refs[:5]
    xt_ref, later_ref, s_ref, h_ref, l_ref, *pt_refs = refs[5:]

    @pl.when(pl.program_id(0) == 0)
    def _():
        at = 0
        for ref in x_refs:
            xt_ref[:, at : at + ref.shape[0]] = ref[...].T
            at += ref.shape[0]
        for p_ref, pt_ref in zip(p_refs, pt_refs):
            pt_ref[...] = p_ref[...].T

    stack(later_refs, later_ref)
    s_ref[...] = dot(xt_ref[...], later_ref[...])
    for pt_ref, above_ref in zip(pt_refs, above_refs):
        s_ref[...] = s_ref[...] - dot(pt_ref[...], above_ref[...])
    for b in range(blocks):
        mine = slice(b * BLK, (b + 1) * BLK)
        s = s_ref[mine, :]
        if b:
            done = slice(0, b * BLK)
            s = s - dot3(
                (lh_ref[mine, done], ll_ref[mine, done]), (h_ref[done, :], l_ref[done, :])
            )
        u = dot3((vh_ref[b], vl_ref[b]), split(s))
        h, l = split(u)
        h_ref[mine, :] = h
        l_ref[mine, :] = l
        out_ref[mine, :] = h


def rows(x, later, above, factors):
    width = x[0][2]
    blocks, band = width // BLK, len(above)
    count = sum(a.shape[0] for a, _, _ in x)
    steps = NB - 1 - band

    def whole(a):
        return pl.BlockSpec(a.shape, lambda i, n=a.ndim: (0,) * n)

    def moving(height, c):
        return pl.BlockSpec((height, width), lambda i: (0, c + i))

    operands = [a for a, _, _ in x] + [a for a, _, _ in later] + [a for a, _ in above] * 2 + factors
    specs = [at_block((a.shape[0], width), 0, c) for a, c, _ in x]
    specs += [moving(a.shape[0], c) for a, c, _ in later]
    specs += [at_block((width, width), 0, c) for _, c in above]
    specs += [moving(width, c + 1) for _, c in above]
    specs += [whole(a) for a in factors]
    return pl.pallas_call(
        functools.partial(rows_kernel, len(x), band, blocks),
        out_shape=jax.ShapeDtypeStruct((width, width * steps), bf16),
        grid=(steps,),
        in_specs=specs,
        out_specs=moving(width, 0),
        scratch_shapes=[
            pltpu.VMEM((width, count), bf16),
            pltpu.VMEM((count, width), bf16),
            pltpu.VMEM((width, width), f32),
            pltpu.VMEM((width, width), bf16),
            pltpu.VMEM((width, width), bf16),
        ]
        + [pltpu.VMEM((width, width), bf16)] * band,
        compiler_params=pltpu.CompilerParams(vmem_limit_bytes=VMEM),
        cost_estimate=pl.CostEstimate(
            flops=8 * width * width * width * steps,
            bytes_accessed=6 * width * width * steps,
            transcendentals=0,
        ),
        name="right_rows",
    )(*operands)


def whiten_kernel(steps, w_ref, *refs):
    *u_refs, out_ref, total_ref = refs
    if steps < NB:
        u_refs = u_refs[:-1]
    at = pl.program_id(0)

    def part(u_ref):
        return lax.dot_general(
            w_ref[...], u_ref[...], (((1,), (1,)), ((), ())), preferred_element_type=f32
        )

    @pl.when(at == 0)
    def _():
        total_ref[...] = part(u_refs[0])

    if steps > 1:

        @pl.when(at > 0)
        def _():
            total_ref[...] += part(u_refs[1])

    @pl.when(at == steps - 1)
    def _():
        out_ref[...] = total_ref[...].astype(bf16)


def whiten(weights, square, right, out):
    height, features = weights.shape
    width = square.shape[0]
    steps = 1 if right is None else 1 + right.shape[1] // width
    band = NB - steps
    operands = [weights, square]
    specs = [pl.BlockSpec((height, width), lambda i: (0, band + i)), at_block((width, width), 0, 0)]
    if steps > 1:
        operands.append(right)
        specs.append(pl.BlockSpec((width, width), lambda i: (0, jnp.maximum(i - 1, 0))))
    aliases = {}
    if out is not None:
        aliases = {len(operands): 0}
        operands.append(out)
        specs.append(pl.BlockSpec(memory_space=pl.ANY))
    return pl.pallas_call(
        functools.partial(whiten_kernel, steps),
        out_shape=jax.ShapeDtypeStruct((height, features), bf16),
        grid=(steps,),
        in_specs=specs,
        out_specs=at_block((height, width), 0, band),
        scratch_shapes=[pltpu.VMEM((height, width), f32)],
        input_output_aliases=aliases,
        compiler_params=pltpu.CompilerParams(vmem_limit_bytes=VMEM),
        cost_estimate=pl.CostEstimate(
            flops=2 * height * width * width * steps,
            bytes_accessed=4 * height * width * steps,
            transcendentals=0,
        ),
        name="whiten",
    )(*operands)


def local(tokens, routes, weights):
    devices = lax.axis_size("tok")
    slices = devices // E
    tok_rows, features = tokens.shape
    most_rows = tok_rows * 5 // 16
    slot_cap = most_rows // slices
    width = features // NB

    picked = routes.reshape(-1)
    onehot = (picked[:, None] == jnp.arange(E, dtype=jnp.int32)[None, :]).astype(jnp.int32)
    before = jnp.cumsum(onehot, axis=0) - onehot
    ranked = jnp.sum(before * onehot, axis=1)
    target = (picked * slices + ranked % slices) * slot_cap + ranked // slices
    slots = devices * slot_cap
    table = (target[None, :] == jnp.arange(slots, dtype=jnp.int32)[:, None]).astype(f32)
    table = jnp.sum(table.reshape(slots, tok_rows, 2), axis=2).astype(bf16)

    def send(values):
        packed = dot(table, values).astype(bf16)
        return lax.all_to_all(packed, "tok", split_axis=0, concat_axis=0, tiled=True)

    def collect(piece):
        pieces = [piece]
        for bit in range(slices.bit_length() - 1):
            route = [(d, d ^ 1 << bit) for d in range(devices)]
            held = pieces[0] if bit == 0 else jnp.concatenate(pieces, 0)
            pieces.append(lax.ppermute(held, "tok", route))
        return pieces

    first = send(tokens[:, :width])
    first, rest = lax.optimization_barrier((first, tokens[:, width:]))
    rest = send(rest)
    first = collect(first)
    x = [(a, 0, width) for a in first]
    square, *factors = diag(x, [])
    rest = collect(rest)
    right, out = [], None
    for band in range(NB):
        above = [(right[b], band - 1 - b) for b in range(band)]
        if band:
            x = [(a, band - 1, width) for a in rest]
            square, *factors = diag(x, above)
        here = None
        if band + 1 < NB:
            here = rows(x, [(a, band, width) for a in rest], above, factors)
            right.append(here)
        out = whiten(weights, square, here, out)
    return out


def solution(mesh):
    spec = P(("groups", "tok"), None)
    return jax.shard_map(
        local, mesh=mesh, in_specs=(spec, spec, spec), out_specs=spec, check_vma=False
    )
```

```python
import functools

import jax
import jax.numpy as jnp
from jax import lax
from jax.experimental import pallas as pl
from jax.experimental.pallas import tpu as pltpu
from jax.sharding import PartitionSpec as P

E = 8
NB = 4
BLK = 128
ROWS = 8
VMEM = 56 * 1024 * 1024

damping = 256.0

f32 = jnp.float32
bf16 = jnp.bfloat16


def dot(a, b):
    return jnp.dot(a, b, preferred_element_type=f32)


def dot_t(a, b):
    return lax.dot_general(a, b, (((0,), (0,)), ((), ())), preferred_element_type=f32)


def dot_nt(a, b):
    return lax.dot_general(a, b, (((1,), (1,)), ((), ())), preferred_element_type=f32)


def split(a):
    high = a.astype(bf16)
    return high, (a - high.astype(f32)).astype(bf16)


def dot3(a, b):
    (ah, al), (bh, bl) = a, b
    return dot(ah, bh) + (dot(ah, bl) + dot(al, bh))


def factor_block(load, store):
    groups = BLK // ROWS
    sub = lax.broadcasted_iota(jnp.int32, (ROWS, BLK), 0)
    lane = lax.broadcasted_iota(jnp.int32, (ROWS, BLK), 1)

    def row(x, k):
        return jnp.broadcast_to(x[k : k + 1, :], (ROWS, BLK))

    def col(x, j):
        return jnp.broadcast_to(x[:, j : j + 1], (ROWS, BLK))

    a_rows = [load(g) for g in range(groups)]
    for p in range(groups):
        base = ROWS * p
        panel = (lane >= base) & (lane < base + ROWS)
        cols = [col(a_rows[p], base + c) for c in range(ROWS)]
        e = {(i, c): row(cols[c], i) for c in range(ROWS) for i in range(c + 1)}
        a = jnp.where(panel, (lane == sub + base).astype(f32), a_rows[p])
        m = [row(a, k) for k in range(ROWS)]
        v = jnp.zeros((ROWS, BLK), f32)
        for k in range(0, ROWS, 2):
            p00, p01, p11 = e[k, k], e[k, k + 1], e[k + 1, k + 1]
            det = p00 * p11 - p01 * p01
            r = pltpu.reciprocal(det, approx=True)
            done, later = range(k), range(k + 2, ROWS)
            x = {i: e[i, k] for i in done} | {c: e[k, c] for c in later}
            y = {i: e[i, k + 1] for i in done} | {c: e[k + 1, c] for c in later}
            n0 = {c: p11 * x[c] - p01 * y[c] for c in later}
            n1 = {c: p00 * y[c] - p01 * x[c] for c in later}
            for c in later:
                for i in range(k + 2, c + 1):
                    e[i, c] = e[i, c] - (n0[i] * x[c] + n1[i] * y[c]) * r
            for c in later:
                e[k, c], e[k + 1, c] = n0[c] * r, n1[c] * r
                for i in done:
                    e[i, c] = e[i, c] - (x[i] * e[k, c] + y[i] * e[k + 1, c])
            m0, m1 = p11 * m[k] - p01 * m[k + 1], p00 * m[k + 1] - p01 * m[k]
            v = jnp.where(sub == k, m[k] * lax.rsqrt(p00), v)
            v = jnp.where(sub == k + 1, m1 * lax.rsqrt(p00 * det), v)
            m[k], m[k + 1] = m0 * r, m1 * r
            for i in (*done, *later):
                m[i] = m[i] - (x[i] * m[k] + y[i] * m[k + 1])
        store(p, jnp.where(lane < base + ROWS, v, 0.0))
        for g in range(p + 1, groups):
            t = [col(a_rows[g], base + k) * m[k] for k in range(ROWS)]
            while len(t) > 1:
                t = [x + y for x, y in zip(t[::2], t[1::2])]
            a_rows[g] = jnp.where(panel, 0.0, a_rows[g]) - t[0]


def stack(refs, out_ref):
    at = 0
    for ref in refs:
        out_ref[at : at + ref.shape[0], :] = ref[...]
        at += ref.shape[0]


def diag_kernel(pieces, band, blocks, *refs):
    x_refs, prev_refs, refs = refs[:pieces], refs[pieces : pieces + band], refs[pieces + band :]
    out_ref, vh_ref, vl_ref = refs[:3]
    x_ref, s_ref, d_ref, v_ref, own_ref, left_ref, right_ref, twice_ref = refs[3:]
    width = blocks * BLK
    row_at = lax.broadcasted_iota(jnp.int32, (BLK, width), 0)
    col_at = lax.broadcasted_iota(jnp.int32, (BLK, width), 1)
    stack(x_refs, x_ref)
    for b in range(blocks):
        mine, on = slice(b * BLK, (b + 1) * BLK), slice(b * BLK, width)
        s = dot_t(x_ref[:, mine], x_ref[:, on])
        for prev_ref in prev_refs:
            s = s - dot_t(prev_ref[:, mine], prev_ref[:, on])
        s_ref[mine, on] = s + jnp.where(col_at[:, on] == row_at[:, on] + b * BLK, damping, 0.0)
        if b:
            s_ref[mine, : b * BLK] = jnp.zeros((BLK, b * BLK), f32)
    d_ref[...] = s_ref[:BLK, :BLK]
    own_ref[...] = jnp.zeros_like(own_ref)

    def block(b):
        return pl.ds(pl.multiple_of(b * BLK, BLK), BLK)

    def finish(b):
        own = own_ref[0], own_ref[1]
        row = dot3(own, split(s_ref[block(b), :]))
        out_ref[block(b), :] = jnp.where(col_at >= row_at + b * BLK, row, 0.0).astype(bf16)
        h, l = split(row)
        zero = jnp.zeros((), bf16)
        vh_ref[block(b), :] = jnp.where(col_at < b * BLK, h, zero)
        vl_ref[block(b), :] = jnp.where(col_at < b * BLK, l, zero)
        vh_ref[block(b), block(b)], vl_ref[block(b), block(b)] = own
        return own, h, l

    def step(b, _):
        def load(g):
            return d_ref[ROWS * g : ROWS * (g + 1), :]

        def store(g, v):
            v_ref[ROWS * g : ROWS * (g + 1), :] = v

        factor_block(load, store)

        before = jnp.maximum(b - 1, 0)
        own, h, l = finish(before)
        ready = b > 0
        after = (col_at >= (before + 1) * BLK) & ready
        zero = jnp.zeros((), bf16)
        left_ref[:BLK, :] = jnp.where(after, h, zero)
        left_ref[BLK:, :] = jnp.where(after, l, zero)
        right_ref[:BLK, :] = h
        right_ref[BLK:, :] = l
        right_ref[:BLK, block(before)], right_ref[BLK:, block(before)] = own
        twice_ref[:BLK, :] = right_ref[:BLK, :]
        twice_ref[BLK:, :] = right_ref[:BLK, :]
        gone = (col_at >= before * BLK) & (col_at < (before + 1) * BLK) & ready
        for later in range(1, blocks):
            mine = slice(later * BLK, (later + 1) * BLK)
            s_ref[mine, :] = jnp.where(gone, 0.0, s_ref[mine, :]) - (
                dot_t(left_ref[:, mine], twice_ref[...])
                + dot_t(left_ref[:BLK, mine], right_ref[BLK:, :])
            )

        v = split(v_ref[...])
        own_ref[0], own_ref[1] = v
        nxt = jnp.minimum(b + 1, blocks - 1)
        u = dot3(v, split(s_ref[block(b), block(nxt)]))
        d_ref[...] = s_ref[block(nxt), block(nxt)] - dot3(split(u.T), split(u))
        return 0

    lax.fori_loop(0, blocks, step, 0)
    finish(blocks - 1)


def at_block(shape, r, c):
    return pl.BlockSpec(shape, lambda i: (r, c))


def diag(x, above):
    width = x[0][2]
    blocks = width // BLK
    square = jax.ShapeDtypeStruct((width, width), bf16)
    count = sum(a.shape[0] for a, _, _ in x)
    operands = [a for a, _, _ in x] + [a for a, _ in above]
    specs = [at_block((a.shape[0], width), 0, c) for a, c, _ in x]
    specs += [at_block((width, width), 0, c) for _, c in above]
    return pl.pallas_call(
        functools.partial(diag_kernel, len(x), len(above), blocks),
        out_shape=[square] * 3,
        grid=(1,),
        in_specs=specs,
        out_specs=[at_block((width, width), 0, 0)] * 3,
        scratch_shapes=[
            pltpu.VMEM((count, width), bf16),
            pltpu.VMEM((width, width), f32),
            pltpu.VMEM((BLK, BLK), f32),
            pltpu.VMEM((BLK, BLK), f32),
            pltpu.VMEM((2, BLK, BLK), bf16),
            pltpu.VMEM((2 * BLK, width), bf16),
            pltpu.VMEM((2 * BLK, width), bf16),
            pltpu.VMEM((2 * BLK, width), bf16),
        ],
        compiler_params=pltpu.CompilerParams(vmem_limit_bytes=VMEM),
        cost_estimate=pl.CostEstimate(
            flops=30_000_000_000, bytes_accessed=8 * width * width, transcendentals=0
        ),
        name="diag_factor",
    )(*operands)


def rows_kernel(pieces, band, steps, *refs):
    x_refs, later_refs, refs = refs[:pieces], refs[pieces : 2 * pieces], refs[2 * pieces :]
    p_refs, above_refs, refs = refs[:band], refs[band : 2 * band], refs[2 * band :]
    square_ref, vh_ref, vl_ref, w_ref, w_later_ref = refs[:5]
    out_ref, white_ref, xt_ref, later_ref, s_ref, total_ref, *pt_refs = refs[6 if band else 5 :]

    @pl.when(pl.program_id(0) == 0)
    def _():
        at = 0
        for ref in x_refs:
            xt_ref[:, at : at + ref.shape[0]] = ref[...].T
            at += ref.shape[0]
        for p_ref, pt_ref in zip(p_refs, pt_refs):
            pt_ref[...] = p_ref[...].T

    stack(later_refs, later_ref)
    s_ref[...] = dot(xt_ref[...], later_ref[...])
    for pt_ref, above_ref in zip(pt_refs, above_refs):
        s_ref[...] = s_ref[...] - dot(pt_ref[...], above_ref[...])
    h, l = split(s_ref[...])
    width = s_ref.shape[0]
    for at in range(0, width, 2 * BLK):
        mine, upto = slice(at, at + 2 * BLK), slice(0, at + 2 * BLK)
        u = dot3((vh_ref[mine, upto], vl_ref[mine, upto]), (h[upto, :], l[upto, :]))
        out_ref[mine, :] = u.astype(bf16)
    part = dot_nt(w_later_ref[...], out_ref[...])

    @pl.when(pl.program_id(0) == 0)
    def _():
        total_ref[...] = part + dot_nt(w_ref[...], square_ref[...])

    @pl.when(pl.program_id(0) > 0)
    def _():
        total_ref[...] += part

    @pl.when(pl.program_id(0) == steps - 1)
    def _():
        white_ref[...] = total_ref[...].astype(bf16)


def rows(x, later, above, factors, weights, white):
    width = x[0][2]
    height, features = weights.shape
    band = len(above)
    count = sum(a.shape[0] for a, _, _ in x)
    steps = NB - 1 - band

    def whole(a):
        return pl.BlockSpec(a.shape, lambda i, n=a.ndim: (0,) * n)

    def moving(height, c):
        return pl.BlockSpec((height, width), lambda i: (0, c + i))

    operands = [a for a, _, _ in x] + [a for a, _, _ in later] + [a for a, _ in above] * 2 + factors
    specs = [at_block((a.shape[0], width), 0, c) for a, c, _ in x]
    specs += [moving(a.shape[0], c) for a, c, _ in later]
    specs += [at_block((width, width), 0, c) for _, c in above]
    specs += [moving(width, c + 1) for _, c in above]
    specs += [whole(a) for a in factors]
    operands += [weights, weights]
    specs += [at_block((height, width), 0, band), moving(height, band + 1)]
    aliases = {}
    if band:
        aliases = {len(operands): 1}
        operands.append(white)
        specs.append(pl.BlockSpec(memory_space=pl.ANY))
    return pl.pallas_call(
        functools.partial(rows_kernel, len(x), band, steps),
        out_shape=[
            jax.ShapeDtypeStruct((width, width * steps), bf16),
            jax.ShapeDtypeStruct((height, features), bf16),
        ],
        grid=(steps,),
        in_specs=specs,
        out_specs=[moving(width, 0), at_block((height, width), 0, band)],
        scratch_shapes=[
            pltpu.VMEM((width, count), bf16),
            pltpu.VMEM((count, width), bf16),
            pltpu.VMEM((width, width), f32),
            pltpu.VMEM((height, width), f32),
        ]
        + [pltpu.VMEM((width, width), bf16)] * band,
        input_output_aliases=aliases,
        compiler_params=pltpu.CompilerParams(vmem_limit_bytes=VMEM),
        cost_estimate=pl.CostEstimate(
            flops=8 * width * width * width * steps,
            bytes_accessed=6 * width * width * steps,
            transcendentals=0,
        ),
        name="right_rows",
    )(*operands)


def whiten_kernel(w_ref, u_ref, _, out_ref):
    out_ref[...] = dot_nt(w_ref[...], u_ref[...]).astype(bf16)


def whiten_last(weights, square, out):
    height, features = weights.shape
    width = square.shape[0]
    rows = height // 4
    return pl.pallas_call(
        whiten_kernel,
        out_shape=jax.ShapeDtypeStruct((height, features), bf16),
        grid=(height // rows,),
        in_specs=[
            pl.BlockSpec((rows, width), lambda i: (i, NB - 1)),
            at_block((width, width), 0, 0),
            pl.BlockSpec(memory_space=pl.ANY),
        ],
        out_specs=pl.BlockSpec((rows, width), lambda i: (i, NB - 1)),
        input_output_aliases={2: 0},
        compiler_params=pltpu.CompilerParams(vmem_limit_bytes=VMEM),
        cost_estimate=pl.CostEstimate(
            flops=2 * height * width * width, bytes_accessed=4 * height * width, transcendentals=0
        ),
        name="whiten_last",
    )(weights, square, out)


def local(tokens, routes, weights):
    devices = lax.axis_size("tok")
    slices = devices // E
    tok_rows, features = tokens.shape
    most_rows = tok_rows * 5 // 16
    slot_cap = most_rows // slices
    width = features // NB

    picked = routes.reshape(-1)
    onehot = (picked[:, None] == jnp.arange(E, dtype=jnp.int32)[None, :]).astype(jnp.int32)
    before = jnp.cumsum(onehot, axis=0) - onehot
    ranked = jnp.sum(before * onehot, axis=1)
    target = (picked * slices + ranked % slices) * slot_cap + ranked // slices
    slots = devices * slot_cap
    table = (target[None, :] == jnp.arange(slots, dtype=jnp.int32)[:, None]).astype(f32)
    table = jnp.sum(table.reshape(slots, tok_rows, 2), axis=2).astype(bf16)

    def send(values):
        packed = dot(table, values).astype(bf16)
        return lax.all_to_all(packed, "tok", split_axis=0, concat_axis=0, tiled=True)

    def collect(piece):
        pieces = [piece]
        for bit in range(slices.bit_length() - 1):
            route = [(d, d ^ 1 << bit) for d in range(devices)]
            held = pieces[0] if bit == 0 else jnp.concatenate(pieces, 0)
            pieces.append(lax.ppermute(held, "tok", route))
        return pieces

    first = send(tokens[:, :width])
    first, rest = lax.optimization_barrier((first, tokens[:, width:]))
    rest = send(rest)
    first = collect(first)
    x = [(a, 0, width) for a in first]
    factors = diag(x, [])
    rest, factors = lax.optimization_barrier((rest, factors))
    rest = collect(rest)
    right, out = [], None
    for band in range(NB):
        above = [(right[b], band - 1 - b) for b in range(band)]
        if band:
            x = [(a, band - 1, width) for a in rest]
            factors = diag(x, above)
        if band + 1 < NB:
            later = [(a, band, width) for a in rest]
            here, out = rows(x, later, above, list(factors), weights, out)
            right.append(here)
    return whiten_last(weights, factors[0], out)


def solution(mesh):
    spec = P(("groups", "tok"), None)
    return jax.shard_map(
        local, mesh=mesh, in_specs=(spec, spec, spec), out_specs=spec, check_vma=False
    )
```

```python
import functools

import jax
import jax.numpy as jnp
from jax import lax
from jax.experimental import pallas as pl
from jax.experimental.pallas import tpu as pltpu
from jax.sharding import PartitionSpec as P

E = 8
NB = 4
BLK = 128
ROWS = 8
VMEM = 56 * 1024 * 1024

damping = 256.0

f32 = jnp.float32
bf16 = jnp.bfloat16


def dot(a, b):
    return jnp.dot(a, b, preferred_element_type=f32)


def dot_t(a, b):
    return lax.dot_general(a, b, (((0,), (0,)), ((), ())), preferred_element_type=f32)


def dot_nt(a, b):
    return lax.dot_general(a, b, (((1,), (1,)), ((), ())), preferred_element_type=f32)


def split(a):
    high = a.astype(bf16)
    return high, (a - high.astype(f32)).astype(bf16)


def dot3(a, b):
    (ah, al), (bh, bl) = a, b
    return dot(ah, bh) + (dot(ah, bl) + dot(al, bh))


def factor_block(load, store, pieces):
    groups = BLK // ROWS
    sub = lax.broadcasted_iota(jnp.int32, (ROWS, BLK), 0)
    lane = lax.broadcasted_iota(jnp.int32, (ROWS, BLK), 1)

    def row(x, k):
        return jnp.broadcast_to(x[k : k + 1, :], (ROWS, BLK))

    def col(x, j):
        return jnp.broadcast_to(x[:, j : j + 1], (ROWS, BLK))

    a_rows = [load(g) for g in range(groups)]
    for p in range(groups):
        base = ROWS * p
        panel = (lane >= base) & (lane < base + ROWS)
        cols = [col(a_rows[p], base + c) for c in range(ROWS)]
        e = {(i, c): row(cols[c], i) for c in range(ROWS) for i in range(c + 1)}
        a = jnp.where(panel, (lane == sub + base).astype(f32), a_rows[p])
        m = [row(a, k) for k in range(ROWS)]
        v = jnp.zeros((ROWS, BLK), f32)
        for k in range(0, ROWS, 2):
            p00, p01, p11 = e[k, k], e[k, k + 1], e[k + 1, k + 1]
            det = p00 * p11 - p01 * p01
            r = pltpu.reciprocal(det, approx=True)
            done, later = range(k), range(k + 2, ROWS)
            x = {i: e[i, k] for i in done} | {c: e[k, c] for c in later}
            y = {i: e[i, k + 1] for i in done} | {c: e[k + 1, c] for c in later}
            n0 = {c: p11 * x[c] - p01 * y[c] for c in later}
            n1 = {c: p00 * y[c] - p01 * x[c] for c in later}
            for c in later:
                for i in range(k + 2, c + 1):
                    e[i, c] = e[i, c] - (n0[i] * x[c] + n1[i] * y[c]) * r
            for c in later:
                e[k, c], e[k + 1, c] = n0[c] * r, n1[c] * r
                for i in done:
                    e[i, c] = e[i, c] - (x[i] * e[k, c] + y[i] * e[k + 1, c])
            m0, m1 = p11 * m[k] - p01 * m[k + 1], p00 * m[k + 1] - p01 * m[k]
            v = jnp.where(sub == k, m[k] * lax.rsqrt(p00), v)
            v = jnp.where(sub == k + 1, m1 * lax.rsqrt(p00 * det), v)
            m[k], m[k + 1] = m0 * r, m1 * r
            for i in (*done, *later):
                m[i] = m[i] - (x[i] * m[k] + y[i] * m[k + 1])
        store(p, jnp.where(lane < base + ROWS, v, 0.0))
        if p < len(pieces):
            pieces[p]()
        for g in range(p + 1, groups):
            t = [col(a_rows[g], base + k) * m[k] for k in range(ROWS)]
            while len(t) > 1:
                t = [x + y for x, y in zip(t[::2], t[1::2])]
            a_rows[g] = jnp.where(panel, 0.0, a_rows[g]) - t[0]


def stack(refs, out_ref):
    at = 0
    for ref in refs:
        out_ref[at : at + ref.shape[0], :] = ref[...]
        at += ref.shape[0]


def diag_kernel(pieces, band, blocks, *refs):
    x_refs, prev_refs, refs = refs[:pieces], refs[pieces : pieces + band], refs[pieces + band :]
    out_ref, vh_ref, vl_ref = refs[:3]
    x_ref, s_ref, d_ref, v_ref, own_ref, left_ref, right_ref = refs[3:]
    width = blocks * BLK
    tile = 2 * BLK
    row_at = lax.broadcasted_iota(jnp.int32, (BLK, tile), 0)
    col_at = lax.broadcasted_iota(jnp.int32, (BLK, tile), 1)
    zero = jnp.zeros((), bf16)
    stack(x_refs, x_ref)
    for at in range(0, width, tile):
        mine, on = slice(at, at + tile), slice(at, width)
        s = dot_t(x_ref[:, mine], x_ref[:, on])
        for prev_ref in prev_refs:
            s = s - dot_t(prev_ref[:, mine], prev_ref[:, on])
        eye = lax.broadcasted_iota(jnp.int32, s.shape, 0) == lax.broadcasted_iota(jnp.int32, s.shape, 1)
        s_ref[mine, on] = s + jnp.where(eye, damping, 0.0)
        if at:
            s_ref[mine, :at] = jnp.zeros((tile, at), f32)
    d_ref[...] = s_ref[:BLK, :BLK]
    own_ref[...] = jnp.zeros_like(own_ref)

    def block(b):
        return pl.ds(pl.multiple_of(b * BLK, BLK), BLK)

    def finish(b, at):
        on = slice(at, at + tile)
        sh, sl = split(s_ref[block(b), on])
        row = dot(own_ref[...], jnp.concatenate([sh, sh, sl], 0))
        out_ref[block(b), on] = jnp.where(col_at + at >= row_at + b * BLK, row, 0.0).astype(bf16)
        h, l = split(row)
        for half in range(0, tile, BLK):
            here, part = slice(at + half, at + half + BLK), slice(half, half + BLK)
            own = (at + half) == b * BLK
            hh = jnp.where(own, own_ref[:, :BLK], h[:, part])
            ll = jnp.where(own, own_ref[:, BLK : 2 * BLK], l[:, part])
            upto = (at + half) <= b * BLK
            vh_ref[block(b), here] = jnp.where(upto, hh, zero)
            vl_ref[block(b), here] = jnp.where(upto, ll, zero)
            right_ref[:BLK, here] = hh
            right_ref[BLK : 2 * BLK, here] = hh
            right_ref[2 * BLK :, here] = ll

    def turn(b, ready):
        for at in range(BLK, width, BLK):
            use = (at > b * BLK) & ready
            h = jnp.where(use, right_ref[:BLK, at : at + BLK].T, zero)
            l = jnp.where(use, right_ref[2 * BLK :, at : at + BLK].T, zero)
            here = slice(at, at + BLK)
            left_ref[here, :BLK] = h
            left_ref[here, BLK : 2 * BLK] = l
            left_ref[here, 2 * BLK :] = h

    def below(b, ready, top, height, at):
        mine, on = slice(top, top + height), slice(at, at + tile)
        col = lax.broadcasted_iota(jnp.int32, (height, tile), 1) + at
        gone = (col >= b * BLK) & (col < (b + 1) * BLK) & ready
        s_ref[mine, on] = jnp.where(gone, 0.0, s_ref[mine, on]) - dot(left_ref[mine, :], right_ref[:, on])

    def step(b, _):
        def load(g):
            return d_ref[ROWS * g : ROWS * (g + 1), :]

        def store(g, v):
            v_ref[ROWS * g : ROWS * (g + 1), :] = v

        before, ready = jnp.maximum(b - 1, 0), b > 0
        pieces = [functools.partial(finish, before, at) for at in range(0, width, tile)]
        pieces.append(functools.partial(turn, before, ready))
        height = (width - BLK) // 2
        for at in range(0, width, tile):
            for top in (BLK, BLK + height):
                pieces.append(functools.partial(below, before, ready, top, height, at))
        factor_block(load, store, pieces)

        vh, vl = split(v_ref[...])
        own_ref[:, :BLK], own_ref[:, BLK : 2 * BLK], own_ref[:, 2 * BLK :] = vh, vl, vh
        nxt = jnp.minimum(b + 1, blocks - 1)
        sh, sl = split(s_ref[block(b), block(nxt)])
        u = dot(own_ref[...], jnp.concatenate([sh, sh, sl], 0))
        h, l = split(u)
        th, tl = split(u.T)
        d_ref[...] = s_ref[block(nxt), block(nxt)] - dot(
            jnp.concatenate([th, tl, th], 1), jnp.concatenate([h, h, l], 0)
        )
        return 0

    lax.fori_loop(0, blocks, step, 0)
    for at in range(0, width, tile):
        finish(blocks - 1, at)


def at_block(shape, r, c):
    return pl.BlockSpec(shape, lambda i: (r, c))


def diag(x, above):
    width = x[0][2]
    blocks = width // BLK
    square = jax.ShapeDtypeStruct((width, width), bf16)
    count = sum(a.shape[0] for a, _, _ in x)
    operands = [a for a, _, _ in x] + [a for a, _ in above]
    specs = [at_block((a.shape[0], width), 0, c) for a, c, _ in x]
    specs += [at_block((width, width), 0, c) for _, c in above]
    return pl.pallas_call(
        functools.partial(diag_kernel, len(x), len(above), blocks),
        out_shape=[square] * 3,
        grid=(1,),
        in_specs=specs,
        out_specs=[at_block((width, width), 0, 0)] * 3,
        scratch_shapes=[
            pltpu.VMEM((count, width), bf16),
            pltpu.VMEM((width, width), f32),
            pltpu.VMEM((BLK, BLK), f32),
            pltpu.VMEM((BLK, BLK), f32),
            pltpu.VMEM((BLK, 3 * BLK), bf16),
            pltpu.VMEM((width, 3 * BLK), bf16),
            pltpu.VMEM((3 * BLK, width), bf16),
        ],
        compiler_params=pltpu.CompilerParams(vmem_limit_bytes=VMEM),
        cost_estimate=pl.CostEstimate(
            flops=30_000_000_000, bytes_accessed=8 * width * width, transcendentals=0
        ),
        name="diag_factor",
    )(*operands)


def rows_kernel(pieces, band, steps, *refs):
    x_refs, later_refs, refs = refs[:pieces], refs[pieces : 2 * pieces], refs[2 * pieces :]
    p_refs, above_refs, refs = refs[:band], refs[band : 2 * band], refs[2 * band :]
    square_ref, vh_ref, vl_ref, w_ref, w_later_ref = refs[:5]
    out_ref, white_ref, xt_ref, later_ref, s_ref, total_ref, *pt_refs = refs[6 if band else 5 :]

    @pl.when(pl.program_id(0) == 0)
    def _():
        at = 0
        for ref in x_refs:
            xt_ref[:, at : at + ref.shape[0]] = ref[...].T
            at += ref.shape[0]
        for p_ref, pt_ref in zip(p_refs, pt_refs):
            pt_ref[...] = p_ref[...].T

    stack(later_refs, later_ref)
    s_ref[...] = dot(xt_ref[...], later_ref[...])
    for pt_ref, above_ref in zip(pt_refs, above_refs):
        s_ref[...] = s_ref[...] - dot(pt_ref[...], above_ref[...])
    h, l = split(s_ref[...])
    width = s_ref.shape[0]
    for at in range(0, width, 2 * BLK):
        mine, upto = slice(at, at + 2 * BLK), slice(0, at + 2 * BLK)
        u = dot3((vh_ref[mine, upto], vl_ref[mine, upto]), (h[upto, :], l[upto, :]))
        out_ref[mine, :] = u.astype(bf16)
    part = dot_nt(w_later_ref[...], out_ref[...])

    @pl.when(pl.program_id(0) == 0)
    def _():
        total_ref[...] = part + dot_nt(w_ref[...], square_ref[...])

    @pl.when(pl.program_id(0) > 0)
    def _():
        total_ref[...] += part

    @pl.when(pl.program_id(0) == steps - 1)
    def _():
        white_ref[...] = total_ref[...].astype(bf16)


def rows(x, later, above, factors, weights, white):
    width = x[0][2]
    height, features = weights.shape
    band = len(above)
    count = sum(a.shape[0] for a, _, _ in x)
    steps = NB - 1 - band

    def whole(a):
        return pl.BlockSpec(a.shape, lambda i, n=a.ndim: (0,) * n)

    def moving(height, c):
        return pl.BlockSpec((height, width), lambda i: (0, c + i))

    operands = [a for a, _, _ in x] + [a for a, _, _ in later] + [a for a, _ in above] * 2 + factors
    specs = [at_block((a.shape[0], width), 0, c) for a, c, _ in x]
    specs += [moving(a.shape[0], c) for a, c, _ in later]
    specs += [at_block((width, width), 0, c) for _, c in above]
    specs += [moving(width, c + 1) for _, c in above]
    specs += [whole(a) for a in factors]
    operands += [weights, weights]
    specs += [at_block((height, width), 0, band), moving(height, band + 1)]
    aliases = {}
    if band:
        aliases = {len(operands): 1}
        operands.append(white)
        specs.append(pl.BlockSpec(memory_space=pl.ANY))
    return pl.pallas_call(
        functools.partial(rows_kernel, len(x), band, steps),
        out_shape=[
            jax.ShapeDtypeStruct((width, width * steps), bf16),
            jax.ShapeDtypeStruct((height, features), bf16),
        ],
        grid=(steps,),
        in_specs=specs,
        out_specs=[moving(width, 0), at_block((height, width), 0, band)],
        scratch_shapes=[
            pltpu.VMEM((width, count), bf16),
            pltpu.VMEM((count, width), bf16),
            pltpu.VMEM((width, width), f32),
            pltpu.VMEM((height, width), f32),
        ]
        + [pltpu.VMEM((width, width), bf16)] * band,
        input_output_aliases=aliases,
        compiler_params=pltpu.CompilerParams(vmem_limit_bytes=VMEM),
        cost_estimate=pl.CostEstimate(
            flops=8 * width * width * width * steps,
            bytes_accessed=6 * width * width * steps,
            transcendentals=0,
        ),
        name="right_rows",
    )(*operands)


def whiten_kernel(w_ref, u_ref, _, out_ref):
    out_ref[...] = dot_nt(w_ref[...], u_ref[...]).astype(bf16)


def whiten_last(weights, square, out):
    height, features = weights.shape
    width = square.shape[0]
    rows = height // 4
    return pl.pallas_call(
        whiten_kernel,
        out_shape=jax.ShapeDtypeStruct((height, features), bf16),
        grid=(height // rows,),
        in_specs=[
            pl.BlockSpec((rows, width), lambda i: (i, NB - 1)),
            at_block((width, width), 0, 0),
            pl.BlockSpec(memory_space=pl.ANY),
        ],
        out_specs=pl.BlockSpec((rows, width), lambda i: (i, NB - 1)),
        input_output_aliases={2: 0},
        compiler_params=pltpu.CompilerParams(vmem_limit_bytes=VMEM),
        cost_estimate=pl.CostEstimate(
            flops=2 * height * width * width, bytes_accessed=4 * height * width, transcendentals=0
        ),
        name="whiten_last",
    )(weights, square, out)


def local(tokens, routes, weights):
    devices = lax.axis_size("tok")
    slices = devices // E
    tok_rows, features = tokens.shape
    most_rows = tok_rows * 5 // 16
    slot_cap = most_rows // slices
    width = features // NB

    picked = routes.reshape(-1)
    onehot = (picked[:, None] == jnp.arange(E, dtype=jnp.int32)[None, :]).astype(jnp.int32)
    before = jnp.cumsum(onehot, axis=0) - onehot
    ranked = jnp.sum(before * onehot, axis=1)
    target = (picked * slices + ranked % slices) * slot_cap + ranked // slices
    slots = devices * slot_cap
    table = (target[None, :] == jnp.arange(slots, dtype=jnp.int32)[:, None]).astype(f32)
    table = jnp.sum(table.reshape(slots, tok_rows, 2), axis=2).astype(bf16)

    def send(values):
        packed = dot(table, values).astype(bf16)
        return lax.all_to_all(packed, "tok", split_axis=0, concat_axis=0, tiled=True)

    def collect(piece):
        pieces = [piece]
        for bit in range(slices.bit_length() - 1):
            route = [(d, d ^ 1 << bit) for d in range(devices)]
            held = pieces[0] if bit == 0 else jnp.concatenate(pieces, 0)
            pieces.append(lax.ppermute(held, "tok", route))
        return pieces

    first = send(tokens[:, :width])
    first, rest = lax.optimization_barrier((first, tokens[:, width:]))
    rest = send(rest)
    first = collect(first)
    x = [(a, 0, width) for a in first]
    factors = diag(x, [])
    rest, factors = lax.optimization_barrier((rest, factors))
    rest = collect(rest)
    right, out = [], None
    for band in range(NB):
        above = [(right[b], band - 1 - b) for b in range(band)]
        if band:
            x = [(a, band - 1, width) for a in rest]
            factors = diag(x, above)
        if band + 1 < NB:
            later = [(a, band, width) for a in rest]
            here, out = rows(x, later, above, list(factors), weights, out)
            right.append(here)
    return whiten_last(weights, factors[0], out)


def solution(mesh):
    spec = P(("groups", "tok"), None)
    return jax.shard_map(
        local, mesh=mesh, in_specs=(spec, spec, spec), out_specs=spec, check_vma=False
    )
```

```python
import functools

import jax
import jax.numpy as jnp
from jax import lax
from jax.experimental import pallas as pl
from jax.experimental.pallas import tpu as pltpu
from jax.sharding import PartitionSpec as P

E = 8
NB = 4
BLK = 128
ROWS = 8
VMEM = 56 * 1024 * 1024

damping = 256.0

f32 = jnp.float32
bf16 = jnp.bfloat16


def dot(a, b):
    return jnp.dot(a, b, preferred_element_type=f32)


def dot_t(a, b):
    return lax.dot_general(a, b, (((0,), (0,)), ((), ())), preferred_element_type=f32)


def dot_nt(a, b):
    return lax.dot_general(a, b, (((1,), (1,)), ((), ())), preferred_element_type=f32)


def split(a):
    high = a.astype(bf16)
    return high, (a - high.astype(f32)).astype(bf16)


def dot3(a, b):
    (ah, al), (bh, bl) = a, b
    return dot(ah, bh) + (dot(ah, bl) + dot(al, bh))


def factor_block(load, store, pieces):
    groups = BLK // ROWS
    sub = lax.broadcasted_iota(jnp.int32, (ROWS, BLK), 0)
    lane = lax.broadcasted_iota(jnp.int32, (ROWS, BLK), 1)

    def row(x, k):
        return jnp.broadcast_to(x[k : k + 1, :], (ROWS, BLK))

    def col(x, j):
        return jnp.broadcast_to(x[:, j : j + 1], (ROWS, BLK))

    a_rows = [load(g) for g in range(groups)]
    for p in range(groups):
        base = ROWS * p
        panel = (lane >= base) & (lane < base + ROWS)
        cols = [col(a_rows[p], base + c) for c in range(ROWS)]
        e = {(i, c): row(cols[c], i) for c in range(ROWS) for i in range(c + 1)}
        a = jnp.where(panel, (lane == sub + base).astype(f32), a_rows[p])
        m = [row(a, k) for k in range(ROWS)]
        v = jnp.zeros((ROWS, BLK), f32)
        for k in range(0, ROWS, 2):
            p00, p01, p11 = e[k, k], e[k, k + 1], e[k + 1, k + 1]
            det = p00 * p11 - p01 * p01
            r = pltpu.reciprocal(det, approx=True)
            done, later = range(k), range(k + 2, ROWS)
            x = {i: e[i, k] for i in done} | {c: e[k, c] for c in later}
            y = {i: e[i, k + 1] for i in done} | {c: e[k + 1, c] for c in later}
            n0 = {c: p11 * x[c] - p01 * y[c] for c in later}
            n1 = {c: p00 * y[c] - p01 * x[c] for c in later}
            for c in later:
                for i in range(k + 2, c + 1):
                    e[i, c] = e[i, c] - (n0[i] * x[c] + n1[i] * y[c]) * r
            for c in later:
                e[k, c], e[k + 1, c] = n0[c] * r, n1[c] * r
                for i in done:
                    e[i, c] = e[i, c] - (x[i] * e[k, c] + y[i] * e[k + 1, c])
            m0, m1 = p11 * m[k] - p01 * m[k + 1], p00 * m[k + 1] - p01 * m[k]
            v = jnp.where(sub == k, m[k] * lax.rsqrt(p00), v)
            v = jnp.where(sub == k + 1, m1 * lax.rsqrt(p00 * det), v)
            m[k], m[k + 1] = m0 * r, m1 * r
            for i in (*done, *later):
                m[i] = m[i] - (x[i] * m[k] + y[i] * m[k + 1])
        store(p, jnp.where(lane < base + ROWS, v, 0.0))
        for piece in pieces[p * len(pieces) // groups : (p + 1) * len(pieces) // groups]:
            piece()
        far = min((p + 4) // 2 * 2, groups)
        for g in range(p + 1, far):
            t = [col(a_rows[g], base + k) * m[k] for k in range(ROWS)]
            while len(t) > 1:
                t = [x + y for x, y in zip(t[::2], t[1::2])]
            a_rows[g] = jnp.where(panel, 0.0, a_rows[g]) - t[0]
        if far < groups:
            mine = m[0]
            for k in range(1, ROWS):
                mine = jnp.where(sub == k, m[k], mine)
            empty = jnp.zeros((ROWS, BLK), f32)
            h, l = split(jnp.concatenate([empty, mine] if p % 2 else [mine, empty], 0))

            def at_rows(x):
                top, bottom = p // 2 * 2 * ROWS, BLK - p // 2 * 2 * ROWS - 2 * ROWS
                parts = [jnp.zeros((top, BLK), bf16)] if top else []
                parts += [x] + ([jnp.zeros((bottom, BLK), bf16)] if bottom else [])
                return jnp.concatenate(parts, 0)

            h, l = at_rows(h), at_rows(l)
            ah, al = split(jnp.concatenate(a_rows[far:], 0))
            t = dot(jnp.concatenate([ah, al, ah], 1), jnp.concatenate([h, h, l], 0))
            for g in range(far, groups):
                at = ROWS * (g - far)
                a_rows[g] = jnp.where(panel, 0.0, a_rows[g]) - t[at : at + ROWS, :]


def stack(refs, out_ref):
    at = 0
    for ref in refs:
        out_ref[at : at + ref.shape[0], :] = ref[...]
        at += ref.shape[0]


def diag_kernel(pieces, band, blocks, *refs):
    x_refs, prev_refs, refs = refs[:pieces], refs[pieces : pieces + band], refs[pieces + band :]
    if band:
        weights_ref, square_ref, beside_ref, _, *refs = refs
        *refs, w_ref, total_ref, sem = refs
        weights_copy = pltpu.make_async_copy(
            weights_ref.at[:, weights_ref.shape[1] - w_ref.shape[1] :], w_ref, sem
        )
        weights_copy.start()
        white_ref = refs.pop(3)
    out_ref, vh_ref, vl_ref = refs[:3]
    x_ref, s_ref, d_ref, v_ref, own_ref, left_ref, right_ref = refs[3:]
    width = blocks * BLK
    tile = 2 * BLK
    row_at = lax.broadcasted_iota(jnp.int32, (BLK, tile), 0)
    col_at = lax.broadcasted_iota(jnp.int32, (BLK, tile), 1)
    zero = jnp.zeros((), bf16)
    stack(x_refs, x_ref)
    for at in range(0, width, tile):
        mine, on = slice(at, at + tile), slice(at, width)
        s = dot_t(x_ref[:, mine], x_ref[:, on])
        for prev_ref in prev_refs:
            s = s - dot_t(prev_ref[:, mine], prev_ref[:, on])
        eye = lax.broadcasted_iota(jnp.int32, s.shape, 0) == lax.broadcasted_iota(jnp.int32, s.shape, 1)
        s_ref[mine, on] = s + jnp.where(eye, damping, 0.0)
        if at:
            s_ref[mine, :at] = jnp.zeros((tile, at), f32)
    d_ref[...] = s_ref[:BLK, :BLK]
    own_ref[...] = jnp.zeros_like(own_ref)

    def block(b):
        return pl.ds(pl.multiple_of(b * BLK, BLK), BLK)

    def finish(b, at):
        on = slice(at, at + tile)
        sh, sl = split(s_ref[block(b), on])
        row = dot(own_ref[...], jnp.concatenate([sh, sh, sl], 0))
        out_ref[block(b), on] = jnp.where(col_at + at >= row_at + b * BLK, row, 0.0).astype(bf16)
        h, l = split(row)
        for half in range(0, tile, BLK):
            here, part = slice(at + half, at + half + BLK), slice(half, half + BLK)
            own = (at + half) == b * BLK
            hh = jnp.where(own, own_ref[:, :BLK], h[:, part])
            ll = jnp.where(own, own_ref[:, BLK : 2 * BLK], l[:, part])
            upto = (at + half) <= b * BLK
            vh_ref[block(b), here] = jnp.where(upto, hh, zero)
            vl_ref[block(b), here] = jnp.where(upto, ll, zero)
            right_ref[:BLK, here] = hh
            right_ref[BLK : 2 * BLK, here] = hh
            right_ref[2 * BLK :, here] = ll

    def turn(b, ready):
        for at in range(BLK, width, BLK):
            use = (at > b * BLK) & ready
            h = jnp.where(use, right_ref[:BLK, at : at + BLK].T, zero)
            l = jnp.where(use, right_ref[2 * BLK :, at : at + BLK].T, zero)
            here = slice(at, at + BLK)
            left_ref[here, :BLK] = h
            left_ref[here, BLK : 2 * BLK] = l
            left_ref[here, 2 * BLK :] = h

    def below(b, ready, top, height, at):
        mine, on = slice(top, top + height), slice(at, at + tile)
        col = lax.broadcasted_iota(jnp.int32, (height, tile), 1) + at
        gone = (col >= b * BLK) & (col < (b + 1) * BLK) & ready
        s_ref[mine, on] = jnp.where(gone, 0.0, s_ref[mine, on]) - dot(left_ref[mine, :], right_ref[:, on])

    def white(b, later, top, height):
        rows_, on = slice(top, top + height), slice((later - 1) * width, later * width)
        u = beside_ref[block(b), on] if later else square_ref[block(b), :]
        part = dot_nt(w_ref[rows_, later * width : (later + 1) * width], u)
        if later:
            part = total_ref[rows_, :] + part
        if later == w_ref.shape[1] // width - 1:
            white_ref[rows_, block(b)] = part.astype(bf16)
        else:
            total_ref[rows_, :] = part

    def step(b, _):
        def load(g):
            return d_ref[ROWS * g : ROWS * (g + 1), :]

        def store(g, v):
            v_ref[ROWS * g : ROWS * (g + 1), :] = v

        before, ready = jnp.maximum(b - 1, 0), b > 0
        pieces = [functools.partial(finish, before, at) for at in range(0, width, tile)]
        pieces.append(functools.partial(turn, before, ready))
        height = (width - BLK) // 2
        for at in range(0, width, tile):
            for top in (BLK, BLK + height):
                pieces.append(functools.partial(below, before, ready, top, height, at))
        if band:
            half = w_ref.shape[0] // 2
            for later in range(w_ref.shape[1] // width):
                pieces += [functools.partial(white, b, later, top, half) for top in (0, half)]
        factor_block(load, store, pieces)

        vh, vl = split(v_ref[...])
        own_ref[:, :BLK], own_ref[:, BLK : 2 * BLK], own_ref[:, 2 * BLK :] = vh, vl, vh
        nxt = jnp.minimum(b + 1, blocks - 1)
        sh, sl = split(s_ref[block(b), block(nxt)])
        u = dot(own_ref[...], jnp.concatenate([sh, sh, sl], 0))
        h, l = split(u)
        th, tl = split(u.T)
        d_ref[...] = s_ref[block(nxt), block(nxt)] - dot(
            jnp.concatenate([th, tl, th], 1), jnp.concatenate([h, h, l], 0)
        )
        return 0

    if band:
        weights_copy.wait()
    lax.fori_loop(0, blocks, step, 0)
    for at in range(0, width, tile):
        finish(blocks - 1, at)


def at_block(shape, r, c):
    return pl.BlockSpec(shape, lambda i: (r, c))


def diag(x, above, weights=None, square=None, out=None):
    width = x[0][2]
    blocks = width // BLK
    count = sum(a.shape[0] for a, _, _ in x)
    operands = [a for a, _, _ in x] + [a for a, _ in above]
    specs = [at_block((a.shape[0], width), 0, c) for a, c, _ in x]
    specs += [at_block((width, width), 0, c) for _, c in above]
    shapes = [jax.ShapeDtypeStruct((width, width), bf16)] * 3
    out_specs = [at_block((width, width), 0, 0)] * 3
    scratch, aliases = [], {}
    if above:
        height, features = weights.shape
        beside = above[-1][0]
        if out is not None:
            aliases = {len(operands) + 3: 3}
        operands += [weights, square, beside, weights if out is None else out]
        anywhere = pl.BlockSpec(memory_space=pl.ANY)
        specs += [anywhere, at_block(square.shape, 0, 0), at_block(beside.shape, 0, 0), anywhere]
        shapes.append(jax.ShapeDtypeStruct((height, features), bf16))
        out_specs.append(at_block((height, width), 0, len(above) - 1))
        scratch = [
            pltpu.VMEM((height, width + beside.shape[1]), bf16),
            pltpu.VMEM((height, BLK), f32),
            pltpu.SemaphoreType.DMA,
        ]
    return pl.pallas_call(
        functools.partial(diag_kernel, len(x), len(above), blocks),
        out_shape=shapes,
        grid=(1,),
        in_specs=specs,
        out_specs=out_specs,
        scratch_shapes=[
            pltpu.VMEM((count, width), bf16),
            pltpu.VMEM((width, width), f32),
            pltpu.VMEM((BLK, BLK), f32),
            pltpu.VMEM((BLK, BLK), f32),
            pltpu.VMEM((BLK, 3 * BLK), bf16),
            pltpu.VMEM((width, 3 * BLK), bf16),
            pltpu.VMEM((3 * BLK, width), bf16),
        ]
        + scratch,
        input_output_aliases=aliases,
        compiler_params=pltpu.CompilerParams(vmem_limit_bytes=VMEM),
        cost_estimate=pl.CostEstimate(
            flops=30_000_000_000, bytes_accessed=8 * width * width, transcendentals=0
        ),
        name="diag_factor",
    )(*operands)


def rows_kernel(pieces, band, *refs):
    x_refs, later_refs, refs = refs[:pieces], refs[pieces : 2 * pieces], refs[2 * pieces :]
    p_refs, above_refs, refs = refs[:band], refs[band : 2 * band], refs[2 * band :]
    vh_ref, vl_ref, out_ref, xt_ref, later_ref, s_ref, *pt_refs = refs

    @pl.when(pl.program_id(0) == 0)
    def _():
        at = 0
        for ref in x_refs:
            xt_ref[:, at : at + ref.shape[0]] = ref[...].T
            at += ref.shape[0]
        for p_ref, pt_ref in zip(p_refs, pt_refs):
            pt_ref[...] = p_ref[...].T

    stack(later_refs, later_ref)
    s_ref[...] = dot(xt_ref[...], later_ref[...])
    for pt_ref, above_ref in zip(pt_refs, above_refs):
        s_ref[...] = s_ref[...] - dot(pt_ref[...], above_ref[...])
    h, l = split(s_ref[...])
    width = s_ref.shape[0]
    for at in range(0, width, 2 * BLK):
        mine, upto = slice(at, at + 2 * BLK), slice(0, at + 2 * BLK)
        u = dot3((vh_ref[mine, upto], vl_ref[mine, upto]), (h[upto, :], l[upto, :]))
        out_ref[mine, :] = u.astype(bf16)


def rows(x, later, above, factors):
    width = x[0][2]
    band = len(above)
    count = sum(a.shape[0] for a, _, _ in x)
    steps = NB - 1 - band

    def whole(a):
        return pl.BlockSpec(a.shape, lambda i, n=a.ndim: (0,) * n)

    def moving(height, c):
        return pl.BlockSpec((height, width), lambda i: (0, c + i))

    operands = [a for a, _, _ in x] + [a for a, _, _ in later] + [a for a, _ in above] * 2 + factors
    specs = [at_block((a.shape[0], width), 0, c) for a, c, _ in x]
    specs += [moving(a.shape[0], c) for a, c, _ in later]
    specs += [at_block((width, width), 0, c) for _, c in above]
    specs += [moving(width, c + 1) for _, c in above]
    specs += [whole(a) for a in factors]
    return pl.pallas_call(
        functools.partial(rows_kernel, len(x), band),
        out_shape=jax.ShapeDtypeStruct((width, width * steps), bf16),
        grid=(steps,),
        in_specs=specs,
        out_specs=moving(width, 0),
        scratch_shapes=[
            pltpu.VMEM((width, count), bf16),
            pltpu.VMEM((count, width), bf16),
            pltpu.VMEM((width, width), f32),
        ]
        + [pltpu.VMEM((width, width), bf16)] * band,
        compiler_params=pltpu.CompilerParams(vmem_limit_bytes=VMEM),
        cost_estimate=pl.CostEstimate(
            flops=8 * width * width * width * steps,
            bytes_accessed=6 * width * width * steps,
            transcendentals=0,
        ),
        name="right_rows",
    )(*operands)


def whiten_kernel(w_ref, u_ref, _, out_ref):
    out_ref[...] = dot_nt(w_ref[...], u_ref[...]).astype(bf16)


def whiten_last(weights, square, out):
    height, features = weights.shape
    width = square.shape[0]
    rows = height // 4
    return pl.pallas_call(
        whiten_kernel,
        out_shape=jax.ShapeDtypeStruct((height, features), bf16),
        grid=(height // rows,),
        in_specs=[
            pl.BlockSpec((rows, width), lambda i: (i, NB - 1)),
            at_block((width, width), 0, 0),
            pl.BlockSpec(memory_space=pl.ANY),
        ],
        out_specs=pl.BlockSpec((rows, width), lambda i: (i, NB - 1)),
        input_output_aliases={2: 0},
        compiler_params=pltpu.CompilerParams(vmem_limit_bytes=VMEM),
        cost_estimate=pl.CostEstimate(
            flops=2 * height * width * width, bytes_accessed=4 * height * width, transcendentals=0
        ),
        name="whiten_last",
    )(weights, square, out)


def local(tokens, routes, weights):
    devices = lax.axis_size("tok")
    slices = devices // E
    tok_rows, features = tokens.shape
    most_rows = tok_rows * 5 // 16
    slot_cap = most_rows // slices
    width = features // NB

    picked = routes.reshape(-1)
    onehot = (picked[:, None] == jnp.arange(E, dtype=jnp.int32)[None, :]).astype(jnp.int32)
    before = jnp.cumsum(onehot, axis=0) - onehot
    ranked = jnp.sum(before * onehot, axis=1)
    target = (picked * slices + ranked % slices) * slot_cap + ranked // slices
    slots = devices * slot_cap
    table = (target[None, :] == jnp.arange(slots, dtype=jnp.int32)[:, None]).astype(f32)
    table = jnp.sum(table.reshape(slots, tok_rows, 2), axis=2).astype(bf16)

    def send(values):
        packed = dot(table, values).astype(bf16)
        return lax.all_to_all(packed, "tok", split_axis=0, concat_axis=0, tiled=True)

    def collect(piece):
        pieces = [piece]
        for bit in range(slices.bit_length() - 1):
            route = [(d, d ^ 1 << bit) for d in range(devices)]
            held = pieces[0] if bit == 0 else jnp.concatenate(pieces, 0)
            pieces.append(lax.ppermute(held, "tok", route))
        return pieces

    first = send(tokens[:, :width])
    first, rest = lax.optimization_barrier((first, tokens[:, width:]))
    rest = send(rest)
    first = collect(first)
    x = [(a, 0, width) for a in first]
    factors = diag(x, [])
    rest, factors = lax.optimization_barrier((rest, factors))
    rest = collect(rest)
    right, out = [], None
    for band in range(NB):
        above = [(right[b], band - 1 - b) for b in range(band)]
        if band:
            x = [(a, band - 1, width) for a in rest]
            *factors, out = diag(x, above, weights, factors[0], out)
        if band + 1 < NB:
            later = [(a, band, width) for a in rest]
            right.append(rows(x, later, above, list(factors[1:])))
    return whiten_last(weights, factors[0], out)


def solution(mesh):
    spec = P(("groups", "tok"), None)
    return jax.shard_map(
        local, mesh=mesh, in_specs=(spec, spec, spec), out_specs=spec, check_vma=False
    )
```

```python
import functools

import jax
import jax.numpy as jnp
from jax import lax
from jax.experimental import pallas as pl
from jax.experimental.pallas import tpu as pltpu
from jax.sharding import PartitionSpec as P

E = 8
NB = 4
BLK = 128
ROWS = 8
SHRINK = 2.0**-16
VMEM = 56 * 1024 * 1024

damping = 256.0

f32 = jnp.float32
bf16 = jnp.bfloat16


def dot(a, b):
    return jnp.dot(a, b, preferred_element_type=f32)


def dot_t(a, b):
    return lax.dot_general(a, b, (((0,), (0,)), ((), ())), preferred_element_type=f32)


def dot_nt(a, b):
    return lax.dot_general(a, b, (((1,), (1,)), ((), ())), preferred_element_type=f32)


def split(a):
    high = a.astype(bf16)
    return high, (a - high.astype(f32)).astype(bf16)


def dot3(a, b):
    (ah, al), (bh, bl) = a, b
    return dot(ah, bh) + (dot(ah, bl) + dot(al, bh))


def factor_block(load, store, pieces):
    groups = BLK // ROWS
    sub = lax.broadcasted_iota(jnp.int32, (ROWS, BLK), 0)
    lane = lax.broadcasted_iota(jnp.int32, (ROWS, BLK), 1)

    def row(x, k):
        return jnp.broadcast_to(x[k : k + 1, :], (ROWS, BLK))

    def col(x, j):
        return jnp.broadcast_to(x[:, j : j + 1], (ROWS, BLK))

    def total(t):
        while len(t) > 1:
            t = [x + y for x, y in zip(t[::2], t[1::2])]
        return t[0]

    a_rows = [load(g) for g in range(groups)]
    cols = [col(a_rows[0], c) for c in range(ROWS)]
    for p in range(groups):
        base = ROWS * p
        panel = (lane >= base) & (lane < base + ROWS)
        e = {(i, c): row(cols[c], i) for c in range(ROWS) for i in range(c + 1)}
        a = jnp.where(panel, (lane == sub + base).astype(f32), a_rows[p])
        m = [row(a, k) for k in range(ROWS)]
        sides = [m]
        if p + 1 < groups:
            beside = [col(a_rows[p + 1], base + c) for c in range(ROWS)]
            cols = [col(a_rows[p + 1], base + ROWS + c) for c in range(ROWS)]
            next_m = list(beside)
            sides.append(next_m)
        v = jnp.zeros((ROWS, BLK), f32)
        scale = scale_r = None
        for k in range(0, ROWS, 2):
            p00, p01, p11 = e[k, k], e[k, k + 1], e[k + 1, k + 1]
            det = p00 * p11 - p01 * p01
            r = pltpu.reciprocal(det, approx=True)
            done, later = range(k), range(k + 2, ROWS)
            soon = range(k + 2, k + 4) if scale is None else ()
            x = {i: e[i, k] for i in done} | {c: e[k, c] for c in later}
            y = {i: e[i, k + 1] for i in done} | {c: e[k + 1, c] for c in later}
            n0 = {c: p11 * x[c] - p01 * y[c] for c in later}
            n1 = {c: p00 * y[c] - p01 * x[c] for c in later}
            if scale is None:
                next_scale, whole_r = det * SHRINK, r
                small_x, small_y = ({c: t[c] * SHRINK for c in later} for t in (x, y))
            else:
                whole_r = r * scale_r
            for c in later:
                for i in range(k + 2, c + 1):
                    if i in soon:
                        e[i, c] = next_scale * e[i, c] - (n0[i] * small_x[c] + n1[i] * small_y[c])
                    else:
                        e[i, c] = e[i, c] - (n0[i] * x[c] + n1[i] * y[c]) * whole_r
            for c in later:
                e[k, c], e[k + 1, c] = n0[c] * r, n1[c] * r
                for i in done:
                    e[i, c] = e[i, c] - (x[i] * e[k, c] + y[i] * e[k + 1, c])
            for side in sides:
                m0, m1 = p11 * side[k] - p01 * side[k + 1], p00 * side[k + 1] - p01 * side[k]
                if side is m:
                    if scale is None:
                        v0, v1 = lax.rsqrt(p00), lax.rsqrt(p00 * det)
                    else:
                        v0 = lax.rsqrt(p00 * scale)
                        v1 = v0 * lax.rsqrt(det)
                    v = jnp.where(sub == k, m[k] * v0, v)
                    v = jnp.where(sub == k + 1, m1 * v1, v)
                side[k], side[k + 1] = m0 * r, m1 * r
                for i in done:
                    side[i] = side[i] - (x[i] * side[k] + y[i] * side[k + 1])
                for i in later:
                    if i in soon:
                        side[i] = next_scale * side[i] - (small_x[i] * m0 + small_y[i] * m1)
                    elif scale is None:
                        side[i] = side[i] - (x[i] * side[k] + y[i] * side[k + 1])
                    else:
                        side[i] = side[i] - (x[i] * side[k] + y[i] * side[k + 1]) * scale_r
            scale, scale_r = (next_scale, r * (1.0 / SHRINK)) if scale is None else (None, None)
        if p + 1 < groups:
            for c in range(ROWS):
                cols[c] = cols[c] - total([beside[k] * row(next_m[k], c) for k in range(ROWS)])
        store(p, jnp.where(lane < base + ROWS, v, 0.0))
        for piece in pieces[p * len(pieces) // groups : (p + 1) * len(pieces) // groups]:
            piece()
        far = min((p + 4) // 2 * 2, groups)
        for g in range(p + 1, far):
            c = beside if g == p + 1 else [col(a_rows[g], base + k) for k in range(ROWS)]
            a_rows[g] = jnp.where(panel, 0.0, a_rows[g]) - total([c[k] * m[k] for k in range(ROWS)])
        if far < groups:
            mine = m[0]
            for k in range(1, ROWS):
                mine = jnp.where(sub == k, m[k], mine)
            empty = jnp.zeros((ROWS, BLK), f32)
            h, l = split(jnp.concatenate([empty, mine] if p % 2 else [mine, empty], 0))

            def at_rows(x):
                top, bottom = p // 2 * 2 * ROWS, BLK - p // 2 * 2 * ROWS - 2 * ROWS
                parts = [jnp.zeros((top, BLK), bf16)] if top else []
                parts += [x] + ([jnp.zeros((bottom, BLK), bf16)] if bottom else [])
                return jnp.concatenate(parts, 0)

            h, l = at_rows(h), at_rows(l)
            ah, al = split(jnp.concatenate(a_rows[far:], 0))
            t = dot(jnp.concatenate([ah, al, ah], 1), jnp.concatenate([h, h, l], 0))
            for g in range(far, groups):
                at = ROWS * (g - far)
                a_rows[g] = jnp.where(panel, 0.0, a_rows[g]) - t[at : at + ROWS, :]


def stack(refs, out_ref):
    at = 0
    for ref in refs:
        out_ref[at : at + ref.shape[0], :] = ref[...]
        at += ref.shape[0]


def diag_kernel(pieces, band, blocks, *refs):
    x_refs, prev_refs, refs = refs[:pieces], refs[pieces : pieces + band], refs[pieces + band :]
    if band:
        weights_ref, square_ref, beside_ref, _, *refs = refs
        *refs, w_ref, total_ref, sem = refs
        weights_copy = pltpu.make_async_copy(
            weights_ref.at[:, weights_ref.shape[1] - w_ref.shape[1] :], w_ref, sem
        )
        weights_copy.start()
        white_ref = refs.pop(3)
    out_ref, vh_ref, vl_ref = refs[:3]
    x_ref, s_ref, d_ref, v_ref, own_ref, left_ref, right_ref = refs[3:]
    width = blocks * BLK
    tile = 2 * BLK
    row_at = lax.broadcasted_iota(jnp.int32, (BLK, tile), 0)
    col_at = lax.broadcasted_iota(jnp.int32, (BLK, tile), 1)
    zero = jnp.zeros((), bf16)
    stack(x_refs, x_ref)
    for at in range(0, width, tile):
        mine, on = slice(at, at + tile), slice(at, width)
        s = dot_t(x_ref[:, mine], x_ref[:, on])
        for prev_ref in prev_refs:
            s = s - dot_t(prev_ref[:, mine], prev_ref[:, on])
        eye = lax.broadcasted_iota(jnp.int32, s.shape, 0) == lax.broadcasted_iota(jnp.int32, s.shape, 1)
        s_ref[mine, on] = s + jnp.where(eye, damping, 0.0)
        if at:
            s_ref[mine, :at] = jnp.zeros((tile, at), f32)
    d_ref[...] = s_ref[:BLK, :BLK]
    own_ref[...] = jnp.zeros_like(own_ref)

    def block(b):
        return pl.ds(pl.multiple_of(b * BLK, BLK), BLK)

    def finish(b, at):
        on = slice(at, at + tile)
        sh, sl = split(s_ref[block(b), on])
        row = dot(own_ref[...], jnp.concatenate([sh, sh, sl], 0))
        out_ref[block(b), on] = jnp.where(col_at + at >= row_at + b * BLK, row, 0.0).astype(bf16)
        h, l = split(row)
        for half in range(0, tile, BLK):
            here, part = slice(at + half, at + half + BLK), slice(half, half + BLK)
            own = (at + half) == b * BLK
            hh = jnp.where(own, own_ref[:, :BLK], h[:, part])
            ll = jnp.where(own, own_ref[:, BLK : 2 * BLK], l[:, part])
            upto = (at + half) <= b * BLK
            vh_ref[block(b), here] = jnp.where(upto, hh, zero)
            vl_ref[block(b), here] = jnp.where(upto, ll, zero)
            right_ref[:BLK, here] = hh
            right_ref[BLK : 2 * BLK, here] = hh
            right_ref[2 * BLK :, here] = ll

    def turn(b, ready):
        for at in range(BLK, width, BLK):
            use = (at > b * BLK) & ready
            h = jnp.where(use, right_ref[:BLK, at : at + BLK].T, zero)
            l = jnp.where(use, right_ref[2 * BLK :, at : at + BLK].T, zero)
            here = slice(at, at + BLK)
            left_ref[here, :BLK] = h
            left_ref[here, BLK : 2 * BLK] = l
            left_ref[here, 2 * BLK :] = h

    def below(b, ready, top, height, at):
        mine, on = slice(top, top + height), slice(at, at + tile)
        col = lax.broadcasted_iota(jnp.int32, (height, tile), 1) + at
        gone = (col >= b * BLK) & (col < (b + 1) * BLK) & ready
        s_ref[mine, on] = jnp.where(gone, 0.0, s_ref[mine, on]) - dot(left_ref[mine, :], right_ref[:, on])

    def white(b, later, top, height):
        rows_, on = slice(top, top + height), slice((later - 1) * width, later * width)
        u = beside_ref[block(b), on] if later else square_ref[block(b), :]
        part = dot_nt(w_ref[rows_, later * width : (later + 1) * width], u)
        if later:
            part = total_ref[rows_, :] + part
        if later == w_ref.shape[1] // width - 1:
            white_ref[rows_, block(b)] = part.astype(bf16)
        else:
            total_ref[rows_, :] = part

    def step(b, _):
        def load(g):
            return d_ref[ROWS * g : ROWS * (g + 1), :]

        def store(g, v):
            v_ref[ROWS * g : ROWS * (g + 1), :] = v

        before, ready = jnp.maximum(b - 1, 0), b > 0
        pieces = [functools.partial(finish, before, at) for at in range(0, width, tile)]
        pieces.append(functools.partial(turn, before, ready))
        height = (width - BLK) // 2
        for at in range(0, width, tile):
            for top in (BLK, BLK + height):
                pieces.append(functools.partial(below, before, ready, top, height, at))
        if band:
            half = w_ref.shape[0] // 2
            for later in range(w_ref.shape[1] // width):
                pieces += [functools.partial(white, b, later, top, half) for top in (0, half)]
        factor_block(load, store, pieces)

        vh, vl = split(v_ref[...])
        own_ref[:, :BLK], own_ref[:, BLK : 2 * BLK], own_ref[:, 2 * BLK :] = vh, vl, vh
        nxt = jnp.minimum(b + 1, blocks - 1)
        sh, sl = split(s_ref[block(b), block(nxt)])
        u = dot(own_ref[...], jnp.concatenate([sh, sh, sl], 0))
        h, l = split(u)
        th, tl = split(u.T)
        d_ref[...] = s_ref[block(nxt), block(nxt)] - dot(
            jnp.concatenate([th, tl, th], 1), jnp.concatenate([h, h, l], 0)
        )
        return 0

    if band:
        weights_copy.wait()
    lax.fori_loop(0, blocks, step, 0)
    for at in range(0, width, tile):
        finish(blocks - 1, at)


def at_block(shape, r, c):
    return pl.BlockSpec(shape, lambda i: (r, c))


def diag(x, above, weights=None, square=None, out=None):
    width = x[0][2]
    blocks = width // BLK
    count = sum(a.shape[0] for a, _, _ in x)
    operands = [a for a, _, _ in x] + [a for a, _ in above]
    specs = [at_block((a.shape[0], width), 0, c) for a, c, _ in x]
    specs += [at_block((width, width), 0, c) for _, c in above]
    shapes = [jax.ShapeDtypeStruct((width, width), bf16)] * 3
    out_specs = [at_block((width, width), 0, 0)] * 3
    scratch, aliases = [], {}
    if above:
        height, features = weights.shape
        beside = above[-1][0]
        if out is not None:
            aliases = {len(operands) + 3: 3}
        operands += [weights, square, beside, weights if out is None else out]
        anywhere = pl.BlockSpec(memory_space=pl.ANY)
        specs += [anywhere, at_block(square.shape, 0, 0), at_block(beside.shape, 0, 0), anywhere]
        shapes.append(jax.ShapeDtypeStruct((height, features), bf16))
        out_specs.append(at_block((height, width), 0, len(above) - 1))
        scratch = [
            pltpu.VMEM((height, width + beside.shape[1]), bf16),
            pltpu.VMEM((height, BLK), f32),
            pltpu.SemaphoreType.DMA,
        ]
    return pl.pallas_call(
        functools.partial(diag_kernel, len(x), len(above), blocks),
        out_shape=shapes,
        grid=(1,),
        in_specs=specs,
        out_specs=out_specs,
        scratch_shapes=[
            pltpu.VMEM((count, width), bf16),
            pltpu.VMEM((width, width), f32),
            pltpu.VMEM((BLK, BLK), f32),
            pltpu.VMEM((BLK, BLK), f32),
            pltpu.VMEM((BLK, 3 * BLK), bf16),
            pltpu.VMEM((width, 3 * BLK), bf16),
            pltpu.VMEM((3 * BLK, width), bf16),
        ]
        + scratch,
        input_output_aliases=aliases,
        compiler_params=pltpu.CompilerParams(vmem_limit_bytes=VMEM),
        cost_estimate=pl.CostEstimate(
            flops=30_000_000_000, bytes_accessed=8 * width * width, transcendentals=0
        ),
        name="diag_factor",
    )(*operands)


def rows_kernel(pieces, band, *refs):
    x_refs, later_refs, refs = refs[:pieces], refs[pieces : 2 * pieces], refs[2 * pieces :]
    p_refs, above_refs, refs = refs[:band], refs[band : 2 * band], refs[2 * band :]
    vh_ref, vl_ref, out_ref, xt_ref, later_ref, s_ref, *pt_refs = refs

    @pl.when(pl.program_id(0) == 0)
    def _():
        at = 0
        for ref in x_refs:
            xt_ref[:, at : at + ref.shape[0]] = ref[...].T
            at += ref.shape[0]
        for p_ref, pt_ref in zip(p_refs, pt_refs):
            pt_ref[...] = p_ref[...].T

    stack(later_refs, later_ref)
    s_ref[...] = dot(xt_ref[...], later_ref[...])
    for pt_ref, above_ref in zip(pt_refs, above_refs):
        s_ref[...] = s_ref[...] - dot(pt_ref[...], above_ref[...])
    h, l = split(s_ref[...])
    width = s_ref.shape[0]
    for at in range(0, width, 2 * BLK):
        mine, upto = slice(at, at + 2 * BLK), slice(0, at + 2 * BLK)
        u = dot3((vh_ref[mine, upto], vl_ref[mine, upto]), (h[upto, :], l[upto, :]))
        out_ref[mine, :] = u.astype(bf16)


def rows(x, later, above, factors):
    width = x[0][2]
    band = len(above)
    count = sum(a.shape[0] for a, _, _ in x)
    steps = NB - 1 - band

    def whole(a):
        return pl.BlockSpec(a.shape, lambda i, n=a.ndim: (0,) * n)

    def moving(height, c):
        return pl.BlockSpec((height, width), lambda i: (0, c + i))

    operands = [a for a, _, _ in x] + [a for a, _, _ in later] + [a for a, _ in above] * 2 + factors
    specs = [at_block((a.shape[0], width), 0, c) for a, c, _ in x]
    specs += [moving(a.shape[0], c) for a, c, _ in later]
    specs += [at_block((width, width), 0, c) for _, c in above]
    specs += [moving(width, c + 1) for _, c in above]
    specs += [whole(a) for a in factors]
    return pl.pallas_call(
        functools.partial(rows_kernel, len(x), band),
        out_shape=jax.ShapeDtypeStruct((width, width * steps), bf16),
        grid=(steps,),
        in_specs=specs,
        out_specs=moving(width, 0),
        scratch_shapes=[
            pltpu.VMEM((width, count), bf16),
            pltpu.VMEM((count, width), bf16),
            pltpu.VMEM((width, width), f32),
        ]
        + [pltpu.VMEM((width, width), bf16)] * band,
        compiler_params=pltpu.CompilerParams(vmem_limit_bytes=VMEM),
        cost_estimate=pl.CostEstimate(
            flops=8 * width * width * width * steps,
            bytes_accessed=6 * width * width * steps,
            transcendentals=0,
        ),
        name="right_rows",
    )(*operands)


def whiten_kernel(w_ref, u_ref, _, out_ref):
    out_ref[...] = dot_nt(w_ref[...], u_ref[...]).astype(bf16)


def whiten_last(weights, square, out):
    height, features = weights.shape
    width = square.shape[0]
    rows = height // 4
    return pl.pallas_call(
        whiten_kernel,
        out_shape=jax.ShapeDtypeStruct((height, features), bf16),
        grid=(height // rows,),
        in_specs=[
            pl.BlockSpec((rows, width), lambda i: (i, NB - 1)),
            at_block((width, width), 0, 0),
            pl.BlockSpec(memory_space=pl.ANY),
        ],
        out_specs=pl.BlockSpec((rows, width), lambda i: (i, NB - 1)),
        input_output_aliases={2: 0},
        compiler_params=pltpu.CompilerParams(vmem_limit_bytes=VMEM),
        cost_estimate=pl.CostEstimate(
            flops=2 * height * width * width, bytes_accessed=4 * height * width, transcendentals=0
        ),
        name="whiten_last",
    )(weights, square, out)


def local(tokens, routes, weights):
    devices = lax.axis_size("tok")
    slices = devices // E
    tok_rows, features = tokens.shape
    most_rows = tok_rows * 5 // 16
    slot_cap = most_rows // slices
    width = features // NB

    picked = routes.reshape(-1)
    onehot = (picked[:, None] == jnp.arange(E, dtype=jnp.int32)[None, :]).astype(jnp.int32)
    before = jnp.cumsum(onehot, axis=0) - onehot
    ranked = jnp.sum(before * onehot, axis=1)
    target = (picked * slices + ranked % slices) * slot_cap + ranked // slices
    slots = devices * slot_cap
    table = (target[None, :] == jnp.arange(slots, dtype=jnp.int32)[:, None]).astype(f32)
    table = jnp.sum(table.reshape(slots, tok_rows, 2), axis=2).astype(bf16)

    def send(values):
        packed = dot(table, values).astype(bf16)
        return lax.all_to_all(packed, "tok", split_axis=0, concat_axis=0, tiled=True)

    def collect(piece):
        pieces = [piece]
        for bit in range(slices.bit_length() - 1):
            route = [(d, d ^ 1 << bit) for d in range(devices)]
            held = pieces[0] if bit == 0 else jnp.concatenate(pieces, 0)
            pieces.append(lax.ppermute(held, "tok", route))
        return pieces

    first = send(tokens[:, :width])
    first, rest = lax.optimization_barrier((first, tokens[:, width:]))
    rest = send(rest)
    first = collect(first)
    x = [(a, 0, width) for a in first]
    factors = diag(x, [])
    rest, factors = lax.optimization_barrier((rest, factors))
    rest = collect(rest)
    right, out = [], None
    for band in range(NB):
        above = [(right[b], band - 1 - b) for b in range(band)]
        if band:
            x = [(a, band - 1, width) for a in rest]
            *factors, out = diag(x, above, weights, factors[0], out)
        if band + 1 < NB:
            later = [(a, band, width) for a in rest]
            right.append(rows(x, later, above, list(factors[1:])))
    return whiten_last(weights, factors[0], out)


def solution(mesh):
    spec = P(("groups", "tok"), None)
    return jax.shard_map(
        local, mesh=mesh, in_specs=(spec, spec, spec), out_specs=spec, check_vma=False
    )
```

```python
import functools

import jax
import jax.numpy as jnp
from jax import lax
from jax.experimental import pallas as pl
from jax.experimental.pallas import tpu as pltpu
from jax.sharding import PartitionSpec as P

E = 8
NB = 4
BLK = 128
ROWS = 8
SHRINK = 2.0**-16
VMEM = 56 * 1024 * 1024

damping = 256.0

f32 = jnp.float32
bf16 = jnp.bfloat16


def dot(a, b):
    return jnp.dot(a, b, preferred_element_type=f32)


def dot_t(a, b):
    return lax.dot_general(a, b, (((0,), (0,)), ((), ())), preferred_element_type=f32)


def dot_nt(a, b):
    return lax.dot_general(a, b, (((1,), (1,)), ((), ())), preferred_element_type=f32)


def split(a):
    high = a.astype(bf16)
    return high, (a - high.astype(f32)).astype(bf16)


def dot3(a, b):
    (ah, al), (bh, bl) = a, b
    return dot(ah, bh) + (dot(ah, bl) + dot(al, bh))


def factor_block(load, store, pieces):
    groups = BLK // ROWS
    sub = lax.broadcasted_iota(jnp.int32, (ROWS, BLK), 0)
    lane = lax.broadcasted_iota(jnp.int32, (ROWS, BLK), 1)

    def row(x, k):
        return jnp.broadcast_to(x[k : k + 1, :], (ROWS, BLK))

    def col(x, j):
        return jnp.broadcast_to(x[:, j : j + 1], (ROWS, BLK))

    def total(t):
        while len(t) > 1:
            t = [x + y for x, y in zip(t[::2], t[1::2])]
        return t[0]

    a_rows = [load(g) for g in range(groups)]
    cols = [col(a_rows[0], c) for c in range(ROWS)]
    for p in range(groups):
        base = ROWS * p
        panel = (lane >= base) & (lane < base + ROWS)
        e = {(i, c): row(cols[c], i) for c in range(ROWS) for i in range(c + 1)}
        a = jnp.where(panel, (lane == sub + base).astype(f32), a_rows[p])
        m = [row(a, k) for k in range(ROWS)]
        sides = [m]
        if p + 1 < groups:
            beside = [col(a_rows[p + 1], base + c) for c in range(ROWS)]
            cols = [col(a_rows[p + 1], base + ROWS + c) for c in range(ROWS)]
            next_m = list(beside)
            sides.append(next_m)
        v = jnp.zeros((ROWS, BLK), f32)
        scale = scale_r = None
        for k in range(0, ROWS, 2):
            p00, p01, p11 = e[k, k], e[k, k + 1], e[k + 1, k + 1]
            det = p00 * p11 - p01 * p01
            r = pltpu.reciprocal(det, approx=True)
            done, later = range(k), range(k + 2, ROWS)
            soon = range(k + 2, k + 4) if scale is None else ()
            x = {i: e[i, k] for i in done} | {c: e[k, c] for c in later}
            y = {i: e[i, k + 1] for i in done} | {c: e[k + 1, c] for c in later}
            n0 = {c: p11 * x[c] - p01 * y[c] for c in later}
            n1 = {c: p00 * y[c] - p01 * x[c] for c in later}
            if scale is None:
                next_scale, whole_r = det * SHRINK, r
                small_x, small_y = ({c: t[c] * SHRINK for c in later} for t in (x, y))
            else:
                whole_r = r * scale_r
            for c in later:
                for i in range(k + 2, c + 1):
                    if i in soon:
                        e[i, c] = next_scale * e[i, c] - (n0[i] * small_x[c] + n1[i] * small_y[c])
                    else:
                        e[i, c] = e[i, c] - (n0[i] * x[c] + n1[i] * y[c]) * whole_r
            for c in later:
                e[k, c], e[k + 1, c] = n0[c] * r, n1[c] * r
                for i in done:
                    e[i, c] = e[i, c] - (x[i] * e[k, c] + y[i] * e[k + 1, c])
            for side in sides:
                m0, m1 = p11 * side[k] - p01 * side[k + 1], p00 * side[k + 1] - p01 * side[k]
                if side is m:
                    if scale is None:
                        v0, v1 = lax.rsqrt(p00), lax.rsqrt(p00 * det)
                    else:
                        v0 = lax.rsqrt(p00 * scale)
                        v1 = v0 * lax.rsqrt(det)
                    v = jnp.where(sub == k, m[k] * v0, v)
                    v = jnp.where(sub == k + 1, m1 * v1, v)
                side[k], side[k + 1] = m0 * r, m1 * r
                for i in done:
                    side[i] = side[i] - (x[i] * side[k] + y[i] * side[k + 1])
                for i in later:
                    if i in soon:
                        side[i] = next_scale * side[i] - (small_x[i] * m0 + small_y[i] * m1)
                    elif scale is None:
                        side[i] = side[i] - (x[i] * side[k] + y[i] * side[k + 1])
                    else:
                        side[i] = side[i] - (x[i] * side[k] + y[i] * side[k + 1]) * scale_r
            scale, scale_r = (next_scale, r * (1.0 / SHRINK)) if scale is None else (None, None)
        if p + 1 < groups:
            for c in range(ROWS):
                cols[c] = cols[c] - total([beside[k] * row(next_m[k], c) for k in range(ROWS)])
        store(p, jnp.where(lane < base + ROWS, v, 0.0))
        for piece in pieces[p * len(pieces) // groups : (p + 1) * len(pieces) // groups]:
            piece()
        far = min((p + 4) // 2 * 2, groups)
        for g in range(p + 1, far):
            c = beside if g == p + 1 else [col(a_rows[g], base + k) for k in range(ROWS)]
            a_rows[g] = jnp.where(panel, 0.0, a_rows[g]) - total([c[k] * m[k] for k in range(ROWS)])
        if far < groups:
            mine = m[0]
            for k in range(1, ROWS):
                mine = jnp.where(sub == k, m[k], mine)
            empty = jnp.zeros((ROWS, BLK), f32)
            h, l = split(jnp.concatenate([empty, mine] if p % 2 else [mine, empty], 0))

            def at_rows(x):
                top, bottom = p // 2 * 2 * ROWS, BLK - p // 2 * 2 * ROWS - 2 * ROWS
                parts = [jnp.zeros((top, BLK), bf16)] if top else []
                parts += [x] + ([jnp.zeros((bottom, BLK), bf16)] if bottom else [])
                return jnp.concatenate(parts, 0)

            h, l = at_rows(h), at_rows(l)
            ah, al = split(jnp.concatenate(a_rows[far:], 0))
            t = dot(jnp.concatenate([ah, al, ah], 1), jnp.concatenate([h, h, l], 0))
            for g in range(far, groups):
                at = ROWS * (g - far)
                a_rows[g] = jnp.where(panel, 0.0, a_rows[g]) - t[at : at + ROWS, :]


def stack(refs, out_ref):
    at = 0
    for ref in refs:
        out_ref[at : at + ref.shape[0], :] = ref[...]
        at += ref.shape[0]


def diag_kernel(pieces, band, blocks, *refs):
    x_refs, prev_refs, refs = refs[:pieces], refs[pieces : pieces + band], refs[pieces + band :]
    if band:
        weights_ref, square_ref, beside_ref, _, *refs = refs
        *refs, w_ref, total_ref, sem = refs
        weights_copy = pltpu.make_async_copy(
            weights_ref.at[:, weights_ref.shape[1] - w_ref.shape[1] :], w_ref, sem
        )
        weights_copy.start()
        white_ref = refs.pop(3)
    out_ref, vh_ref, vl_ref = refs[:3]
    x_ref, s_ref, d_ref, v_ref, own_ref, left_ref, right_ref = refs[3:]
    width = blocks * BLK
    tile = 2 * BLK
    row_at = lax.broadcasted_iota(jnp.int32, (BLK, tile), 0)
    col_at = lax.broadcasted_iota(jnp.int32, (BLK, tile), 1)
    zero = jnp.zeros((), bf16)
    stack(x_refs, x_ref)
    for at in range(0, width, tile):
        mine, on = slice(at, at + tile), slice(at, width)
        s = dot_t(x_ref[:, mine], x_ref[:, on])
        for prev_ref in prev_refs:
            s = s - dot_t(prev_ref[:, mine], prev_ref[:, on])
        eye = lax.broadcasted_iota(jnp.int32, s.shape, 0) == lax.broadcasted_iota(jnp.int32, s.shape, 1)
        s_ref[mine, on] = s + jnp.where(eye, damping, 0.0)
        if at:
            s_ref[mine, :at] = jnp.zeros((tile, at), f32)
    d_ref[...] = s_ref[:BLK, :BLK]
    own_ref[...] = jnp.zeros_like(own_ref)

    def block(b):
        return pl.ds(pl.multiple_of(b * BLK, BLK), BLK)

    def finish(b, at):
        on = slice(at, at + tile)
        sh, sl = split(s_ref[block(b), on])
        row = dot(own_ref[...], jnp.concatenate([sh, sh, sl], 0))
        out_ref[block(b), on] = jnp.where(col_at + at >= row_at + b * BLK, row, 0.0).astype(bf16)
        h, l = split(row)
        for half in range(0, tile, BLK):
            here, part = slice(at + half, at + half + BLK), slice(half, half + BLK)
            own = (at + half) == b * BLK
            hh = jnp.where(own, own_ref[:, :BLK], h[:, part])
            ll = jnp.where(own, own_ref[:, BLK : 2 * BLK], l[:, part])
            upto = (at + half) <= b * BLK
            vh_ref[block(b), here] = jnp.where(upto, hh, zero)
            vl_ref[block(b), here] = jnp.where(upto, ll, zero)
            right_ref[:BLK, here] = hh
            right_ref[BLK : 2 * BLK, here] = hh
            right_ref[2 * BLK :, here] = ll

    def turn(b, ready):
        for at in range(BLK, width, BLK):
            use = (at > b * BLK) & ready
            h = jnp.where(use, right_ref[:BLK, at : at + BLK].T, zero)
            l = jnp.where(use, right_ref[2 * BLK :, at : at + BLK].T, zero)
            here = slice(at, at + BLK)
            left_ref[here, :BLK] = h
            left_ref[here, BLK : 2 * BLK] = l
            left_ref[here, 2 * BLK :] = h

    def below(b, ready, top, height, at):
        mine, on = slice(top, top + height), slice(at, at + tile)
        col = lax.broadcasted_iota(jnp.int32, (height, tile), 1) + at
        gone = (col >= b * BLK) & (col < (b + 1) * BLK) & ready
        s_ref[mine, on] = jnp.where(gone, 0.0, s_ref[mine, on]) - dot(left_ref[mine, :], right_ref[:, on])

    def white(b, later, top, height):
        half = w_ref.shape[0] // 2
        rows_ = pl.ds(pl.multiple_of(b % 2 * half + top, height), height)
        mine, on = pl.ds(pl.multiple_of(b // 2 * tile, tile), tile), slice((later - 1) * width, later * width)
        held = slice(top, top + height)
        u = beside_ref[mine, on] if later else square_ref[mine, :]
        part = dot_nt(w_ref[rows_, later * width : (later + 1) * width], u)
        if later:
            part = total_ref[held, :] + part
        if later == w_ref.shape[1] // width - 1:
            white_ref[rows_, mine] = part.astype(bf16)
        else:
            total_ref[held, :] = part

    def step(b, _):
        def load(g):
            return d_ref[ROWS * g : ROWS * (g + 1), :]

        def store(g, v):
            v_ref[ROWS * g : ROWS * (g + 1), :] = v

        before, ready = jnp.maximum(b - 1, 0), b > 0
        pieces = [functools.partial(finish, before, at) for at in range(0, width, tile)]
        pieces.append(functools.partial(turn, before, ready))
        height = (width - BLK) // 2
        for at in range(0, width, tile):
            for top in (BLK, BLK + height):
                pieces.append(functools.partial(below, before, ready, top, height, at))
        if band:
            part = w_ref.shape[0] // 4
            for later in range(w_ref.shape[1] // width):
                pieces += [functools.partial(white, b, later, top, part) for top in (0, part)]
        factor_block(load, store, pieces)

        vh, vl = split(v_ref[...])
        own_ref[:, :BLK], own_ref[:, BLK : 2 * BLK], own_ref[:, 2 * BLK :] = vh, vl, vh
        nxt = jnp.minimum(b + 1, blocks - 1)
        sh, sl = split(s_ref[block(b), block(nxt)])
        u = dot(own_ref[...], jnp.concatenate([sh, sh, sl], 0))
        h, l = split(u)
        th, tl = split(u.T)
        d_ref[...] = s_ref[block(nxt), block(nxt)] - dot(
            jnp.concatenate([th, tl, th], 1), jnp.concatenate([h, h, l], 0)
        )
        return 0

    if band:
        weights_copy.wait()
    lax.fori_loop(0, blocks, step, 0)
    for at in range(0, width, tile):
        finish(blocks - 1, at)


def at_block(shape, r, c):
    return pl.BlockSpec(shape, lambda i: (r, c))


def diag(x, above, weights=None, square=None, out=None):
    width = x[0][2]
    blocks = width // BLK
    count = sum(a.shape[0] for a, _, _ in x)
    operands = [a for a, _, _ in x] + [a for a, _ in above]
    specs = [at_block((a.shape[0], width), 0, c) for a, c, _ in x]
    specs += [at_block((width, width), 0, c) for _, c in above]
    shapes = [jax.ShapeDtypeStruct((width, width), bf16)] * 3
    out_specs = [at_block((width, width), 0, 0)] * 3
    scratch, aliases = [], {}
    if above:
        height, features = weights.shape
        beside = above[-1][0]
        if out is not None:
            aliases = {len(operands) + 3: 3}
        operands += [weights, square, beside, weights if out is None else out]
        anywhere = pl.BlockSpec(memory_space=pl.ANY)
        specs += [anywhere, at_block(square.shape, 0, 0), at_block(beside.shape, 0, 0), anywhere]
        shapes.append(jax.ShapeDtypeStruct((height, features), bf16))
        out_specs.append(at_block((height, width), 0, len(above) - 1))
        scratch = [
            pltpu.VMEM((height, width + beside.shape[1]), bf16),
            pltpu.VMEM((height // 2, 2 * BLK), f32),
            pltpu.SemaphoreType.DMA,
        ]
    return pl.pallas_call(
        functools.partial(diag_kernel, len(x), len(above), blocks),
        out_shape=shapes,
        grid=(1,),
        in_specs=specs,
        out_specs=out_specs,
        scratch_shapes=[
            pltpu.VMEM((count, width), bf16),
            pltpu.VMEM((width, width), f32),
            pltpu.VMEM((BLK, BLK), f32),
            pltpu.VMEM((BLK, BLK), f32),
            pltpu.VMEM((BLK, 3 * BLK), bf16),
            pltpu.VMEM((width, 3 * BLK), bf16),
            pltpu.VMEM((3 * BLK, width), bf16),
        ]
        + scratch,
        input_output_aliases=aliases,
        compiler_params=pltpu.CompilerParams(vmem_limit_bytes=VMEM),
        cost_estimate=pl.CostEstimate(
            flops=30_000_000_000, bytes_accessed=8 * width * width, transcendentals=0
        ),
        name="diag_factor",
    )(*operands)


def rows_kernel(pieces, band, *refs):
    x_refs, later_refs, refs = refs[:pieces], refs[pieces : 2 * pieces], refs[2 * pieces :]
    p_refs, above_refs, refs = refs[:band], refs[band : 2 * band], refs[2 * band :]
    vh_ref, vl_ref, out_ref, xt_ref, later_ref, s_ref, *pt_refs = refs

    @pl.when(pl.program_id(0) == 0)
    def _():
        at = 0
        for ref in x_refs:
            xt_ref[:, at : at + ref.shape[0]] = ref[...].T
            at += ref.shape[0]
        for p_ref, pt_ref in zip(p_refs, pt_refs):
            pt_ref[...] = p_ref[...].T

    stack(later_refs, later_ref)
    s_ref[...] = dot(xt_ref[...], later_ref[...])
    for pt_ref, above_ref in zip(pt_refs, above_refs):
        s_ref[...] = s_ref[...] - dot(pt_ref[...], above_ref[...])
    h, l = split(s_ref[...])
    width = s_ref.shape[0]
    for at in range(0, width, 2 * BLK):
        mine, upto = slice(at, at + 2 * BLK), slice(0, at + 2 * BLK)
        u = dot3((vh_ref[mine, upto], vl_ref[mine, upto]), (h[upto, :], l[upto, :]))
        out_ref[mine, :] = u.astype(bf16)


def rows(x, later, above, factors):
    width = x[0][2]
    band = len(above)
    count = sum(a.shape[0] for a, _, _ in x)
    steps = NB - 1 - band

    def whole(a):
        return pl.BlockSpec(a.shape, lambda i, n=a.ndim: (0,) * n)

    def moving(height, c):
        return pl.BlockSpec((height, width), lambda i: (0, c + i))

    operands = [a for a, _, _ in x] + [a for a, _, _ in later] + [a for a, _ in above] * 2 + factors
    specs = [at_block((a.shape[0], width), 0, c) for a, c, _ in x]
    specs += [moving(a.shape[0], c) for a, c, _ in later]
    specs += [at_block((width, width), 0, c) for _, c in above]
    specs += [moving(width, c + 1) for _, c in above]
    specs += [whole(a) for a in factors]
    return pl.pallas_call(
        functools.partial(rows_kernel, len(x), band),
        out_shape=jax.ShapeDtypeStruct((width, width * steps), bf16),
        grid=(steps,),
        in_specs=specs,
        out_specs=moving(width, 0),
        scratch_shapes=[
            pltpu.VMEM((width, count), bf16),
            pltpu.VMEM((count, width), bf16),
            pltpu.VMEM((width, width), f32),
        ]
        + [pltpu.VMEM((width, width), bf16)] * band,
        compiler_params=pltpu.CompilerParams(vmem_limit_bytes=VMEM),
        cost_estimate=pl.CostEstimate(
            flops=8 * width * width * width * steps,
            bytes_accessed=6 * width * width * steps,
            transcendentals=0,
        ),
        name="right_rows",
    )(*operands)


def whiten_kernel(w_ref, u_ref, _, out_ref):
    out_ref[...] = dot_nt(w_ref[...], u_ref[...]).astype(bf16)


def whiten_last(weights, square, out):
    height, features = weights.shape
    width = square.shape[0]
    rows = height // 4
    return pl.pallas_call(
        whiten_kernel,
        out_shape=jax.ShapeDtypeStruct((height, features), bf16),
        grid=(height // rows,),
        in_specs=[
            pl.BlockSpec((rows, width), lambda i: (i, NB - 1)),
            at_block((width, width), 0, 0),
            pl.BlockSpec(memory_space=pl.ANY),
        ],
        out_specs=pl.BlockSpec((rows, width), lambda i: (i, NB - 1)),
        input_output_aliases={2: 0},
        compiler_params=pltpu.CompilerParams(vmem_limit_bytes=VMEM),
        cost_estimate=pl.CostEstimate(
            flops=2 * height * width * width, bytes_accessed=4 * height * width, transcendentals=0
        ),
        name="whiten_last",
    )(weights, square, out)


def local(tokens, routes, weights):
    devices = lax.axis_size("tok")
    slices = devices // E
    tok_rows, features = tokens.shape
    most_rows = tok_rows * 5 // 16
    slot_cap = most_rows // slices
    width = features // NB

    picked = routes.reshape(-1)
    onehot = (picked[:, None] == jnp.arange(E, dtype=jnp.int32)[None, :]).astype(jnp.int32)
    before = jnp.cumsum(onehot, axis=0) - onehot
    ranked = jnp.sum(before * onehot, axis=1)
    target = (picked * slices + ranked % slices) * slot_cap + ranked // slices
    slots = devices * slot_cap
    table = (target[None, :] == jnp.arange(slots, dtype=jnp.int32)[:, None]).astype(f32)
    table = jnp.sum(table.reshape(slots, tok_rows, 2), axis=2).astype(bf16)

    def send(values):
        packed = dot(table, values).astype(bf16)
        return lax.all_to_all(packed, "tok", split_axis=0, concat_axis=0, tiled=True)

    def collect(piece):
        pieces = [piece]
        for bit in range(slices.bit_length() - 1):
            route = [(d, d ^ 1 << bit) for d in range(devices)]
            held = pieces[0] if bit == 0 else jnp.concatenate(pieces, 0)
            pieces.append(lax.ppermute(held, "tok", route))
        return pieces

    first = send(tokens[:, :width])
    first, rest = lax.optimization_barrier((first, tokens[:, width:]))
    rest = send(rest)
    first = collect(first)
    x = [(a, 0, width) for a in first]
    factors = diag(x, [])
    rest, factors = lax.optimization_barrier((rest, factors))
    rest = collect(rest)
    right, out = [], None
    for band in range(NB):
        above = [(right[b], band - 1 - b) for b in range(band)]
        if band:
            x = [(a, band - 1, width) for a in rest]
            *factors, out = diag(x, above, weights, factors[0], out)
        if band + 1 < NB:
            later = [(a, band, width) for a in rest]
            right.append(rows(x, later, above, list(factors[1:])))
    return whiten_last(weights, factors[0], out)


def solution(mesh):
    spec = P(("groups", "tok"), None)
    return jax.shard_map(
        local, mesh=mesh, in_specs=(spec, spec, spec), out_specs=spec, check_vma=False
    )
```

```python
import functools

import jax
import jax.numpy as jnp
from jax import lax
from jax.experimental import pallas as pl
from jax.experimental.pallas import tpu as pltpu
from jax.sharding import PartitionSpec as P

E = 8
NB = 4
BLK = 128
ROWS = 8
SHRINK = 2.0**-16
VMEM = 56 * 1024 * 1024

damping = 256.0

f32 = jnp.float32
bf16 = jnp.bfloat16


def dot(a, b):
    return jnp.dot(a, b, preferred_element_type=f32)


def dot_t(a, b):
    return lax.dot_general(a, b, (((0,), (0,)), ((), ())), preferred_element_type=f32)


def dot_nt(a, b):
    return lax.dot_general(a, b, (((1,), (1,)), ((), ())), preferred_element_type=f32)


def split(a):
    high = a.astype(bf16)
    return high, (a - high.astype(f32)).astype(bf16)


def dot3(a, b):
    (ah, al), (bh, bl) = a, b
    return dot(ah, bh) + (dot(ah, bl) + dot(al, bh))


def factor_block(load, store, pieces):
    groups = BLK // ROWS
    sub = lax.broadcasted_iota(jnp.int32, (ROWS, BLK), 0)
    lane = lax.broadcasted_iota(jnp.int32, (ROWS, BLK), 1)

    def row(x, k):
        return jnp.broadcast_to(x[k : k + 1, :], (ROWS, BLK))

    def col(x, j):
        return jnp.broadcast_to(x[:, j : j + 1], (ROWS, BLK))

    def total(t):
        while len(t) > 1:
            t = [x + y for x, y in zip(t[::2], t[1::2])]
        return t[0]

    a_rows = [load(g) for g in range(groups)]
    cols = [col(a_rows[0], c) for c in range(ROWS)]
    for p in range(groups):
        base = ROWS * p
        panel = (lane >= base) & (lane < base + ROWS)
        e = {(i, c): row(cols[c], i) for c in range(ROWS) for i in range(c + 1)}
        a = jnp.where(panel, (lane == sub + base).astype(f32), a_rows[p])
        m = [row(a, k) for k in range(ROWS)]
        sides = [m]
        if p + 1 < groups:
            beside = [col(a_rows[p + 1], base + c) for c in range(ROWS)]
            cols = [col(a_rows[p + 1], base + ROWS + c) for c in range(ROWS)]
            next_m = list(beside)
            sides.append(next_m)
        v = jnp.zeros((ROWS, BLK), f32)
        scale = scale_r = None
        for k in range(0, ROWS, 2):
            p00, p01, p11 = e[k, k], e[k, k + 1], e[k + 1, k + 1]
            det = p00 * p11 - p01 * p01
            r = pltpu.reciprocal(det, approx=True)
            done, later = range(k), range(k + 2, ROWS)
            soon = range(k + 2, k + 4) if scale is None else ()
            x = {i: e[i, k] for i in done} | {c: e[k, c] for c in later}
            y = {i: e[i, k + 1] for i in done} | {c: e[k + 1, c] for c in later}
            n0 = {c: p11 * x[c] - p01 * y[c] for c in later}
            n1 = {c: p00 * y[c] - p01 * x[c] for c in later}
            if scale is None:
                next_scale, whole_r = det * SHRINK, r
                small_x, small_y = ({c: t[c] * SHRINK for c in later} for t in (x, y))
            else:
                whole_r = r * scale_r
            for c in later:
                for i in range(k + 2, c + 1):
                    if i in soon:
                        e[i, c] = next_scale * e[i, c] - (n0[i] * small_x[c] + n1[i] * small_y[c])
                    else:
                        e[i, c] = e[i, c] - (n0[i] * x[c] + n1[i] * y[c]) * whole_r
            for c in later:
                e[k, c], e[k + 1, c] = n0[c] * r, n1[c] * r
                for i in done:
                    e[i, c] = e[i, c] - (x[i] * e[k, c] + y[i] * e[k + 1, c])
            for side in sides:
                m0, m1 = p11 * side[k] - p01 * side[k + 1], p00 * side[k + 1] - p01 * side[k]
                if side is m:
                    if scale is None:
                        v0, v1 = lax.rsqrt(p00), lax.rsqrt(p00 * det)
                    else:
                        v0 = lax.rsqrt(p00 * scale)
                        v1 = v0 * lax.rsqrt(det)
                    v = jnp.where(sub == k, m[k] * v0, v)
                    v = jnp.where(sub == k + 1, m1 * v1, v)
                side[k], side[k + 1] = m0 * r, m1 * r
                for i in done:
                    side[i] = side[i] - (x[i] * side[k] + y[i] * side[k + 1])
                for i in later:
                    if i in soon:
                        side[i] = next_scale * side[i] - (small_x[i] * m0 + small_y[i] * m1)
                    elif scale is None:
                        side[i] = side[i] - (x[i] * side[k] + y[i] * side[k + 1])
                    else:
                        side[i] = side[i] - (x[i] * side[k] + y[i] * side[k + 1]) * scale_r
            scale, scale_r = (next_scale, r * (1.0 / SHRINK)) if scale is None else (None, None)
        if p + 1 < groups:
            for c in range(ROWS):
                cols[c] = cols[c] - total([beside[k] * row(next_m[k], c) for k in range(ROWS)])
        store(p, jnp.where(lane < base + ROWS, v, 0.0))
        for piece in pieces[p * len(pieces) // groups : (p + 1) * len(pieces) // groups]:
            piece()
        far = min((p + 4) // 2 * 2, groups)
        for g in range(p + 1, far):
            c = beside if g == p + 1 else [col(a_rows[g], base + k) for k in range(ROWS)]
            a_rows[g] = jnp.where(panel, 0.0, a_rows[g]) - total([c[k] * m[k] for k in range(ROWS)])
        if far < groups:
            mine = m[0]
            for k in range(1, ROWS):
                mine = jnp.where(sub == k, m[k], mine)
            empty = jnp.zeros((ROWS, BLK), f32)
            h, l = split(jnp.concatenate([empty, mine] if p % 2 else [mine, empty], 0))

            def at_rows(x):
                top, bottom = p // 2 * 2 * ROWS, BLK - p // 2 * 2 * ROWS - 2 * ROWS
                parts = [jnp.zeros((top, BLK), bf16)] if top else []
                parts += [x] + ([jnp.zeros((bottom, BLK), bf16)] if bottom else [])
                return jnp.concatenate(parts, 0)

            h, l = at_rows(h), at_rows(l)
            ah, al = split(jnp.concatenate(a_rows[far:], 0))
            t = dot(jnp.concatenate([ah, al, ah], 1), jnp.concatenate([h, h, l], 0))
            for g in range(far, groups):
                at = ROWS * (g - far)
                a_rows[g] = jnp.where(panel, 0.0, a_rows[g]) - t[at : at + ROWS, :]


def stack(refs, out_ref):
    at = 0
    for ref in refs:
        out_ref[at : at + ref.shape[0], :] = ref[...]
        at += ref.shape[0]


def diag_kernel(pieces, band, blocks, *refs):
    x_refs, prev_refs, refs = refs[:pieces], refs[pieces : pieces + band], refs[pieces + band :]
    if band:
        weights_ref, square_ref, beside_ref, _, *refs = refs
        *refs, w_ref, total_ref, sem = refs
        weights_copy = pltpu.make_async_copy(
            weights_ref.at[:, weights_ref.shape[1] - w_ref.shape[1] :], w_ref, sem
        )
        weights_copy.start()
        white_ref = refs.pop(3)
    out_ref, vh_ref, vl_ref = refs[:3]
    x_ref, s_ref, d_ref, v_ref, own_ref, left_ref, right_ref = refs[3:]
    width = blocks * BLK
    tile = 2 * BLK
    row_at = lax.broadcasted_iota(jnp.int32, (BLK, tile), 0)
    col_at = lax.broadcasted_iota(jnp.int32, (BLK, tile), 1)
    zero = jnp.zeros((), bf16)
    stack(x_refs, x_ref)
    for at in range(0, width, tile):
        mine, on = slice(at, at + tile), slice(at, width)
        s = dot_t(x_ref[:, mine], x_ref[:, on])
        for prev_ref in prev_refs:
            s = s - dot_t(prev_ref[:, mine], prev_ref[:, on])
        eye = lax.broadcasted_iota(jnp.int32, s.shape, 0) == lax.broadcasted_iota(jnp.int32, s.shape, 1)
        s_ref[mine, on] = s + jnp.where(eye, damping, 0.0)
        if at:
            s_ref[mine, :at] = jnp.zeros((tile, at), f32)
    d_ref[...] = s_ref[:BLK, :BLK]
    own_ref[...] = jnp.zeros_like(own_ref)

    def block(b):
        return pl.ds(pl.multiple_of(b * BLK, BLK), BLK)

    def finish(b, at):
        on = slice(at, at + tile)
        sh, sl = split(s_ref[block(b), on])
        row = dot(own_ref[...], jnp.concatenate([sh, sh, sl], 0))
        out_ref[block(b), on] = jnp.where(col_at + at >= row_at + b * BLK, row, 0.0).astype(bf16)
        h, l = split(row)
        for half in range(0, tile, BLK):
            here, part = slice(at + half, at + half + BLK), slice(half, half + BLK)
            own = (at + half) == b * BLK
            hh = jnp.where(own, own_ref[:, :BLK], h[:, part])
            ll = jnp.where(own, own_ref[:, BLK : 2 * BLK], l[:, part])
            upto = (at + half) <= b * BLK
            vh_ref[block(b), here] = jnp.where(upto, hh, zero)
            vl_ref[block(b), here] = jnp.where(upto, ll, zero)
            right_ref[:BLK, here] = hh
            right_ref[BLK : 2 * BLK, here] = hh
            right_ref[2 * BLK :, here] = ll

    def turn(b, ready):
        for at in range(BLK, width, BLK):
            use = (at > b * BLK) & ready
            h = jnp.where(use, right_ref[:BLK, at : at + BLK].T, zero)
            l = jnp.where(use, right_ref[2 * BLK :, at : at + BLK].T, zero)
            here = slice(at, at + BLK)
            left_ref[here, :BLK] = h
            left_ref[here, BLK : 2 * BLK] = l
            left_ref[here, 2 * BLK :] = h

    def below(b, ready, top, height, at):
        mine, on = slice(top, top + height), slice(at, at + tile)
        col = lax.broadcasted_iota(jnp.int32, (height, tile), 1) + at
        gone = (col >= b * BLK) & (col < (b + 1) * BLK) & ready
        s_ref[mine, on] = jnp.where(gone, 0.0, s_ref[mine, on]) - dot(left_ref[mine, :], right_ref[:, on])

    def white(b, later, top, height):
        half = w_ref.shape[0] // 2
        rows_ = pl.ds(pl.multiple_of(b % 2 * half + top, height), height)
        mine, on = pl.ds(pl.multiple_of(b // 2 * tile, tile), tile), slice((later - 1) * width, later * width)
        held = slice(top, top + height)
        u = beside_ref[mine, on] if later else square_ref[mine, :]
        part = dot_nt(w_ref[rows_, later * width : (later + 1) * width], u)
        if later:
            part = total_ref[held, :] + part
        if later == w_ref.shape[1] // width - 1:
            white_ref[rows_, mine] = part.astype(bf16)
        else:
            total_ref[held, :] = part

    def step(b, _):
        def load(g):
            return d_ref[ROWS * g : ROWS * (g + 1), :]

        def store(g, v):
            v_ref[ROWS * g : ROWS * (g + 1), :] = v

        before, ready = jnp.maximum(b - 1, 0), b > 0
        pieces = [functools.partial(finish, before, at) for at in range(0, width, tile)]
        pieces.append(functools.partial(turn, before, ready))
        height = (width - BLK) // 2
        for at in range(0, width, tile):
            for top in (BLK, BLK + height):
                pieces.append(functools.partial(below, before, ready, top, height, at))
        if band:
            part = w_ref.shape[0] // 4
            for later in range(w_ref.shape[1] // width):
                pieces += [functools.partial(white, b, later, top, part) for top in (0, part)]
        factor_block(load, store, pieces)

        vh, vl = split(v_ref[...])
        own_ref[:, :BLK], own_ref[:, BLK : 2 * BLK], own_ref[:, 2 * BLK :] = vh, vl, vh
        nxt = jnp.minimum(b + 1, blocks - 1)
        sh, sl = split(s_ref[block(b), block(nxt)])
        u = dot(own_ref[...], jnp.concatenate([sh, sh, sl], 0))
        h, l = split(u)
        th, tl = split(u.T)
        d_ref[...] = s_ref[block(nxt), block(nxt)] - dot(
            jnp.concatenate([th, tl, th], 1), jnp.concatenate([h, h, l], 0)
        )
        return 0

    if band:
        weights_copy.wait()
    lax.fori_loop(0, blocks, step, 0)
    for at in range(0, width, tile):
        finish(blocks - 1, at)
    if band == NB - 1:
        for top in range(0, w_ref.shape[0], tile):
            mine = slice(top, top + tile)
            white_ref[mine, width:] = dot_nt(w_ref[mine, width:], out_ref[...]).astype(bf16)


def at_block(shape, r, c):
    return pl.BlockSpec(shape, lambda i: (r, c))


def diag(x, above, weights=None, square=None, out=None):
    width = x[0][2]
    blocks = width // BLK
    count = sum(a.shape[0] for a, _, _ in x)
    operands = [a for a, _, _ in x] + [a for a, _ in above]
    specs = [at_block((a.shape[0], width), 0, c) for a, c, _ in x]
    specs += [at_block((width, width), 0, c) for _, c in above]
    shapes = [jax.ShapeDtypeStruct((width, width), bf16)] * 3
    out_specs = [at_block((width, width), 0, 0)] * 3
    scratch, aliases = [], {}
    if above:
        height, features = weights.shape
        beside = above[-1][0]
        if out is not None:
            aliases = {len(operands) + 3: 3}
        operands += [weights, square, beside, weights if out is None else out]
        anywhere = pl.BlockSpec(memory_space=pl.ANY)
        specs += [anywhere, at_block(square.shape, 0, 0), at_block(beside.shape, 0, 0), anywhere]
        shapes.append(jax.ShapeDtypeStruct((height, features), bf16))
        last = len(above) == NB - 1
        out_specs.append(
            at_block((height, 2 * width), 0, NB // 2 - 1) if last else at_block((height, width), 0, len(above) - 1)
        )
        scratch = [
            pltpu.VMEM((height, width + beside.shape[1]), bf16),
            pltpu.VMEM((height // 2, 2 * BLK), f32),
            pltpu.SemaphoreType.DMA,
        ]
    return pl.pallas_call(
        functools.partial(diag_kernel, len(x), len(above), blocks),
        out_shape=shapes,
        grid=(1,),
        in_specs=specs,
        out_specs=out_specs,
        scratch_shapes=[
            pltpu.VMEM((count, width), bf16),
            pltpu.VMEM((width, width), f32),
            pltpu.VMEM((BLK, BLK), f32),
            pltpu.VMEM((BLK, BLK), f32),
            pltpu.VMEM((BLK, 3 * BLK), bf16),
            pltpu.VMEM((width, 3 * BLK), bf16),
            pltpu.VMEM((3 * BLK, width), bf16),
        ]
        + scratch,
        input_output_aliases=aliases,
        compiler_params=pltpu.CompilerParams(vmem_limit_bytes=VMEM),
        cost_estimate=pl.CostEstimate(
            flops=30_000_000_000, bytes_accessed=8 * width * width, transcendentals=0
        ),
        name="diag_factor",
    )(*operands)


def rows_kernel(pieces, band, *refs):
    x_refs, later_refs, refs = refs[:pieces], refs[pieces : 2 * pieces], refs[2 * pieces :]
    p_refs, above_refs, refs = refs[:band], refs[band : 2 * band], refs[2 * band :]
    vh_ref, vl_ref, out_ref, xt_ref, later_ref, s_ref, *pt_refs = refs

    @pl.when(pl.program_id(0) == 0)
    def _():
        at = 0
        for ref in x_refs:
            xt_ref[:, at : at + ref.shape[0]] = ref[...].T
            at += ref.shape[0]
        for p_ref, pt_ref in zip(p_refs, pt_refs):
            pt_ref[...] = p_ref[...].T

    stack(later_refs, later_ref)
    s_ref[...] = dot(xt_ref[...], later_ref[...])
    for pt_ref, above_ref in zip(pt_refs, above_refs):
        s_ref[...] = s_ref[...] - dot(pt_ref[...], above_ref[...])
    h, l = split(s_ref[...])
    width = s_ref.shape[0]
    for at in range(0, width, 2 * BLK):
        mine, upto = slice(at, at + 2 * BLK), slice(0, at + 2 * BLK)
        u = dot3((vh_ref[mine, upto], vl_ref[mine, upto]), (h[upto, :], l[upto, :]))
        out_ref[mine, :] = u.astype(bf16)


def rows(x, later, above, factors):
    width = x[0][2]
    band = len(above)
    count = sum(a.shape[0] for a, _, _ in x)
    steps = NB - 1 - band

    def whole(a):
        return pl.BlockSpec(a.shape, lambda i, n=a.ndim: (0,) * n)

    def moving(height, c):
        return pl.BlockSpec((height, width), lambda i: (0, c + i))

    operands = [a for a, _, _ in x] + [a for a, _, _ in later] + [a for a, _ in above] * 2 + factors
    specs = [at_block((a.shape[0], width), 0, c) for a, c, _ in x]
    specs += [moving(a.shape[0], c) for a, c, _ in later]
    specs += [at_block((width, width), 0, c) for _, c in above]
    specs += [moving(width, c + 1) for _, c in above]
    specs += [whole(a) for a in factors]
    return pl.pallas_call(
        functools.partial(rows_kernel, len(x), band),
        out_shape=jax.ShapeDtypeStruct((width, width * steps), bf16),
        grid=(steps,),
        in_specs=specs,
        out_specs=moving(width, 0),
        scratch_shapes=[
            pltpu.VMEM((width, count), bf16),
            pltpu.VMEM((count, width), bf16),
            pltpu.VMEM((width, width), f32),
        ]
        + [pltpu.VMEM((width, width), bf16)] * band,
        compiler_params=pltpu.CompilerParams(vmem_limit_bytes=VMEM),
        cost_estimate=pl.CostEstimate(
            flops=8 * width * width * width * steps,
            bytes_accessed=6 * width * width * steps,
            transcendentals=0,
        ),
        name="right_rows",
    )(*operands)


def local(tokens, routes, weights):
    devices = lax.axis_size("tok")
    slices = devices // E
    tok_rows, features = tokens.shape
    most_rows = tok_rows * 5 // 16
    slot_cap = most_rows // slices
    width = features // NB

    picked = routes.reshape(-1)
    onehot = (picked[:, None] == jnp.arange(E, dtype=jnp.int32)[None, :]).astype(jnp.int32)
    before = jnp.cumsum(onehot, axis=0) - onehot
    ranked = jnp.sum(before * onehot, axis=1)
    target = (picked * slices + ranked % slices) * slot_cap + ranked // slices
    slots = devices * slot_cap
    table = (target[None, :] == jnp.arange(slots, dtype=jnp.int32)[:, None]).astype(f32)
    table = jnp.sum(table.reshape(slots, tok_rows, 2), axis=2).astype(bf16)

    def pack(values):
        return dot(table, values).astype(bf16).reshape(devices, slot_cap, -1)

    def send(packed):
        received = lax.all_to_all(packed, "tok", split_axis=0, concat_axis=0, tiled=True)
        return received.reshape(slots, -1)

    def collect(piece):
        pieces = [piece]
        for bit in range(slices.bit_length() - 1):
            route = [(d, d ^ 1 << bit) for d in range(devices)]
            held = pieces[0] if bit == 0 else jnp.concatenate(pieces, 0)
            pieces.append(lax.ppermute(held, "tok", route))
        return pieces

    first = send(pack(tokens[:, :width]))
    first, rest = lax.optimization_barrier((first, pack(tokens[:, width:])))
    rest = send(rest)
    first = collect(first)
    x = [(a, 0, width) for a in first]
    factors = diag(x, [])
    rest, factors = lax.optimization_barrier((rest, factors))
    rest = collect(rest)
    right, out = [], None
    for band in range(NB):
        above = [(right[b], band - 1 - b) for b in range(band)]
        if band:
            x = [(a, band - 1, width) for a in rest]
            *factors, out = diag(x, above, weights, factors[0], out)
        if band + 1 < NB:
            later = [(a, band, width) for a in rest]
            right.append(rows(x, later, above, list(factors[1:])))
    return out


def solution(mesh):
    spec = P(("groups", "tok"), None)
    return jax.shard_map(
        local, mesh=mesh, in_specs=(spec, spec, spec), out_specs=spec, check_vma=False
    )
```
